256 devices in a mesh: tm: 8 (over x, core), tile: 32 (over y, z).
Axes of the slice: x: 4, y: 4, z: 8, core: 2. Of those that a mesh axis runs over, the one named last changes fastest.
Arguments:
- recording: bfloat16 [262144, 1024], P('tile', 'tm'), may hold values from -300 to 300
- footprints: bfloat16 [262144, 256], P('tile'), may hold values from -0.375 to 0.375
- pattern: int32 [1024, 4], P('tile'), may hold values from 0 to 35, as said below
- decay: float32 [65536], P('tile'), may hold values from 0.96 to 1
- frame_gain: float32 [1024], P('tm'), may hold values from 0.6 to 1
- spikes: float32 [65536, 1024], P('tile', 'tm'), may hold values from 0 to 0.15
Outputs:
- spikes_out: float32 [65536, 1024], P('tile', 'tm')
- traces_last: float32 [65536, 1024], P('tile', 'tm')
The draws below stay inside these ranges and needn't reach their ends.
Inputs may be any that keep to these rules, and one draw needn't show every extreme that they name: `pattern`: with p = q % 32, row q holds 4 different values between p and p + 4, always including p, p + 2 and p + 4, in some order; value v names the stripe's own neuron block v - 2, so values under 2 or over 2048 // 64 + 1 name edge blocks of the adjacent stripes.
All inputs are finite; a program needn't handle non-finite values.
Results may differ from the reference program's by a relative error of at most 0.00073.
Values may be sent and summed in bfloat16 or wider, within the bound.
A program may use at most 128 MiB of HBM per device.

```python
import math
import jax
import jax.numpy as jnp
from jax import lax

NEU_BLOCK = 64
PIX_BLOCK = 256
K = 4
HB = 2
ITERS = 2
NEU_DEV = 2048
NEURONS = 65536
PIXELS = 262144
FRAMES = 1024
N_TILE = 32


def draw_recording(key, part):
    key_rows, key_cols, key_base = jax.random.split(key, 3)
    row_scale = jnp.exp(jax.random.uniform(key_rows, (PIXELS, 1), jnp.float32, math.log(0.3), math.log(3.0)))
    col_scale = jnp.exp(jax.random.uniform(key_cols, (1, FRAMES), jnp.float32, math.log(0.3), math.log(3.0)))
    pixel_pos = jnp.arange(PIXELS, dtype=jnp.float32)[:, None] / PIXELS - 0.5
    frame_pos = jnp.arange(FRAMES, dtype=jnp.float32)[None, :] / FRAMES - 0.5
    rising = jnp.exp(math.log(3.0) * (pixel_pos + frame_pos))
    values = jax.random.normal(key_base, (PIXELS, FRAMES), jnp.float32) * row_scale * col_scale * rising
    return values.astype(jnp.bfloat16)


def draw_pattern(key, part):
    stripe_blocks = NEU_DEV // NEU_BLOCK
    block_rows = PIXELS // PIX_BLOCK
    local_block = (jnp.arange(block_rows, dtype=jnp.int32) % stripe_blocks).astype(jnp.int32)
    inner = jnp.array([offset for offset in range(1 - HB, HB) if offset != 0], jnp.int32)
    anchors = jnp.array([-HB, 0, HB], jnp.int32)
    row_keys = jax.random.split(key, block_rows)

    def one_row(row_key):
        key_pick, key_order = jax.random.split(row_key)
        extra = jax.random.permutation(key_pick, inner)[:K - 3]
        offsets = jnp.concatenate([anchors, extra])
        return jax.random.permutation(key_order, offsets)
    offsets = jax.vmap(one_row)(row_keys)
    return (local_block[:, None] + HB + offsets).astype(jnp.int32)


def draw_decay(key, part):
    key_kind, key_fast, key_slow = jax.random.split(key, 3)
    share = 0.5
    quick = jax.random.uniform(key_kind, (NEURONS,), jnp.float32) < share
    tau_fast = jnp.exp(jax.random.uniform(key_fast, (NEURONS,), jnp.float32, math.log(30.0), math.log(50.0)))
    tau_slow = jnp.exp(jax.random.uniform(key_slow, (NEURONS,), jnp.float32, math.log(2.0 * FRAMES), math.log(8.0 * FRAMES)))
    tau_all = jnp.where(quick, tau_fast, tau_slow)
    return jnp.exp(-1.0 / tau_all).astype(jnp.float32)


def draw_frame_gain(key, part):
    key_spot, key_level = jax.random.split(key)
    spots = jax.random.choice(key_spot, FRAMES, (3,), replace=False)
    levels = jax.random.uniform(key_level, (3,), jnp.float32, 0.6, 0.8)
    return jnp.ones((FRAMES,), jnp.float32).at[spots].set(levels)


def shard_levels(key, dims, cuts, smallest, largest):
    level = 1.0
    for axis_at, shards_of in cuts:
        draws = jax.random.uniform(jax.random.fold_in(jax.random.fold_in(key, 6), axis_at), (shards_of,), jnp.float32, smallest / len(cuts), largest / len(cuts))
        level = level * jnp.repeat(jnp.exp(draws), dims[axis_at] // shards_of).reshape((-1,) + (1,) * (len(dims) - 1 - axis_at))
    return level


def noise(own_key, dims, scale, reach, cuts=(), kind=jnp.bfloat16):
    entries = scale * jax.random.normal(own_key, dims, jnp.float32)
    if cuts:
        entries = entries * shard_levels(own_key, dims, cuts, -0.22, 0.18)
    return jnp.clip(entries, -reach, reach).astype(kind)


def setup_inputs(seed: int = 0) -> dict:
    streams_of = jax.random.split(jax.random.key(seed), 7)
    return {
        "recording": draw_recording(jax.random.fold_in(streams_of[6], 71), 0),
        "footprints": noise(streams_of[1], (PIXELS, K * NEU_BLOCK), (K * NEU_BLOCK) ** -0.5, 0.375, ((0, 32),)),
        "pattern": draw_pattern(jax.random.fold_in(streams_of[6], 71), 0),
        "decay": draw_decay(jax.random.fold_in(streams_of[6], 71), 0),
        "frame_gain": draw_frame_gain(jax.random.fold_in(streams_of[6], 71), 0),
        "spikes": jnp.clip(0.15 * jax.random.uniform(streams_of[5], (NEURONS, FRAMES), jnp.float32) ** shard_levels(streams_of[5], (NEURONS, FRAMES), ((0, 32), (1, 8)), -0.2, 0.2), 0.0, 0.15),
    }


def forward_filter(drive, decay, frame_gain):

    def advance(state, column):
        source, factor = column
        state = decay * factor * state + source
        return (state, state)
    _, rows_out = lax.scan(advance, jnp.zeros(decay.shape, jnp.float32), (drive.T, frame_gain))
    return rows_out.T

def backward_filter(source, decay, frame_gain):
    next_gain = jnp.concatenate([frame_gain[1:], jnp.zeros((1,), jnp.float32)])

    def retreat(state, column):
        values, factor = column
        state = values + decay * factor * state
        return (state, state)
    _, rows_out = lax.scan(retreat, jnp.zeros(decay.shape, jnp.float32), (source.T, next_gain), reverse=True)
    return rows_out.T

def footprint_apply(values, footprints, pattern):
    stripe_blocks = NEU_DEV // NEU_BLOCK
    total_blocks = NEURONS // NEU_BLOCK
    padded = jnp.pad(values.reshape(total_blocks, NEU_BLOCK, FRAMES), ((HB, HB), (0, 0), (0, 0)))
    stripes = footprints.reshape(N_TILE, stripe_blocks, PIX_BLOCK, K * NEU_BLOCK)
    patterns = pattern.reshape(N_TILE, stripe_blocks, K)

    def one_stripe(items):
        stripe, feet, rows_idx = items
        picked = padded[stripe * stripe_blocks + rows_idx]
        picked = picked.reshape(stripe_blocks, K * NEU_BLOCK, FRAMES).astype(jnp.float32)
        return jnp.einsum('paj,pjf->paf', feet.astype(jnp.float32), picked, precision=lax.Precision.HIGHEST)
    fitted = lax.map(one_stripe, (jnp.arange(N_TILE, dtype=jnp.int32), stripes, patterns))
    return fitted.reshape(PIXELS, FRAMES)

def footprint_adjoint(residual, footprints, pattern):
    stripe_blocks = NEU_DEV // NEU_BLOCK
    total_blocks = NEURONS // NEU_BLOCK
    stripes = footprints.reshape(N_TILE, stripe_blocks, PIX_BLOCK, K * NEU_BLOCK)
    resid_stripes = residual.reshape(N_TILE, stripe_blocks, PIX_BLOCK, FRAMES)
    patterns = pattern.reshape(N_TILE, stripe_blocks, K)

    def one_stripe(totals, items):
        stripe, feet, resid, rows_idx = items
        contrib = jnp.einsum('paj,paf->pjf', feet.astype(jnp.float32), resid.astype(jnp.float32), precision=lax.Precision.HIGHEST)
        contrib = contrib.reshape(stripe_blocks * K, NEU_BLOCK, FRAMES)
        targets = (stripe * stripe_blocks + rows_idx).reshape(-1).astype(jnp.int32)
        return (totals.at[targets].add(contrib), None)
    start = jnp.zeros((total_blocks + 2 * HB, NEU_BLOCK, FRAMES), jnp.float32)
    totals, _ = lax.scan(one_stripe, start, (jnp.arange(N_TILE, dtype=jnp.int32), stripes, resid_stripes, patterns))
    return totals[HB:HB + total_blocks].reshape(NEURONS, FRAMES)

def reference(recording, footprints, pattern, decay, frame_gain, spikes):
    gain = jnp.sqrt(1.0 - decay * decay)[:, None]
    record = recording.astype(jnp.float32)
    current = spikes
    traces = spikes
    for iteration in range(ITERS):
        traces = forward_filter(gain * current, decay, frame_gain)
        fitted = footprint_apply(traces.astype(jnp.bfloat16), footprints, pattern)
        residual = (fitted - record).astype(jnp.bfloat16)
        gradient = gain * backward_filter(footprint_adjoint(residual, footprints, pattern), decay, frame_gain)
        direction = forward_filter(gain * gradient, decay, frame_gain).astype(jnp.bfloat16)
        projected = footprint_apply(direction, footprints, pattern)
        step_size = jnp.sum(gradient * gradient) / (jnp.sum(projected * projected) + 1e-06)
        current = jnp.maximum(current - step_size * gradient, 0.0)
    return (current, traces)
```

```python
import functools
import itertools

import jax
import jax.numpy as jnp
from jax import lax
from jax.experimental import pallas as pl
from jax.experimental.pallas import tpu as pltpu
from jax.sharding import PartitionSpec as P

NEU_BLOCK = 64
PIX_BLOCK = 256
K = 4
HB = 2
ITERS = 2

NX, NY, NZ, NC = 4, 4, 8, 2
NT = NX * NC
NTILE = NY * NZ
FR = 128
NCOL = 18
ROWS = 24
NEU = 2048
PIX = 8192
MESH = pl.DeviceIdType.MESH
F32 = jnp.float32
BF16 = jnp.bfloat16


def ring_distance(d, n):
    return min(d, n - d)


def offsets(keep):
    found = []
    for dx, dy, dz, dc in itertools.product(range(NX), range(NY), range(NZ), range(NC)):
        if (dx, dy, dz, dc) != (0, 0, 0, 0) and keep(dx, dy, dz, dc):
            far = ring_distance(dx, NX) + ring_distance(dy, NY) + ring_distance(dz, NZ)
            found.append((-far, dx, dy, dz, dc))
    return [o[1:] for o in sorted(found)]


TM_GROUP = offsets(lambda dx, dy, dz, dc: dy == 0 and dz == 0)
PLANE_GROUP = offsets(lambda dx, dy, dz, dc: dx == 0 and dc == 0)
STAGES = (TM_GROUP, PLANE_GROUP)


def split_rows(x):
    hi = x.astype(BF16)
    lo = (x - hi.astype(F32)).astype(BF16)
    return hi, lo


def kernel(
    rec_hbm, foot_hbm, pat, decay, fgain, spk_hbm,
    out_spk, out_tr,
    foot_raw, rec_raw, spk_raw, fp, fpt, rec_t,
    cur, grad, fwd, inv, sq, xh, loc, loc2, acc_n, acc_s, val_n, val_s,
    lgb, tri_lo, tri_up, decd, tab_u, tab_e, tab_t, tab_q, tab_c, row_w, row_c,
    halo_spk, halo_dec, msg_a0, msg_a1, msg_cd, got_a0, got_a1, got_cd,
    msg_b, got_b, msg_e, got_e0, got_e1,
    ss, rs, ls,
):
    tm = lax.axis_index("tm")
    tile = lax.axis_index("tile")
    px, pc = lax.div(tm, NC), lax.rem(tm, NC)
    py, pz = lax.div(tile, NZ), lax.rem(tile, NZ)

    def device_at(o):
        dx, dy, dz, dc = o
        x = lax.rem(px + dx, NX) if dx else px
        c = lax.rem(pc + dc, NC) if dc else pc
        y = lax.rem(py + dy, NY) if dy else py
        z = lax.rem(pz + dz, NZ) if dz else pz
        return (x * NC + c, y * NZ + z)

    upper = (tm, lax.rem(tile + 1, NTILE))
    lower = (tm, lax.rem(tile + NTILE - 1, NTILE))

    load_spk = pltpu.make_async_copy(spk_hbm, spk_raw, ls.at[0])
    load_foot = pltpu.make_async_copy(foot_hbm, foot_raw, ls.at[1])
    load_rec = pltpu.make_async_copy(rec_hbm, rec_raw, ls.at[2])
    load_spk.start()
    load_foot.start()
    load_rec.start()

    group = sorted(set(TM_GROUP) | set(STAGES[0]) | set(STAGES[1]))
    barrier = pltpu.get_barrier_semaphore()
    for o in group:
        pl.semaphore_signal(barrier, inc=1, device_id=device_at(o), device_id_type=MESH)
    for d in (upper, lower):
        pl.semaphore_signal(barrier, inc=1, device_id=d, device_id_type=MESH)

    def lanes(c, width=128):
        return pl.ds(pl.multiple_of(c * width, width), width)

    row = lax.broadcasted_iota(jnp.int32, (FR, FR), 0)
    col = lax.broadcasted_iota(jnp.int32, (FR, FR), 1)
    low_half = col < NEU_BLOCK
    t_centred = (row - 63).astype(F32)

    lower_tri = (row >= col).astype(BF16)
    upper_tri = (row <= col).astype(BF16)
    tri_lo[:, :FR] = lower_tri
    tri_lo[:, FR:] = lower_tri
    tri_up[:, :FR] = upper_tri
    tri_up[:, FR:] = upper_tri

    log_fg = jnp.log(fgain[...])
    lg = jnp.sum(jnp.where(row >= col, log_fg, 0.0), axis=1, keepdims=True)
    lg_mid = lg[63:64, :]
    lg_tot = lg[127:128, :]
    lgb[...] = jnp.broadcast_to(lg - lg_mid, (FR, FR))

    msg_a0[...] = jnp.zeros_like(msg_a0)
    msg_a1[...] = jnp.zeros_like(msg_a1)
    msg_cd[...] = jnp.zeros_like(msg_cd)
    msg_a0[ROWS + NCOL : ROWS + NCOL + 1, :] = jnp.broadcast_to(lg_tot, (1, FR))
    msg_a0[ROWS + NCOL + 1 : ROWS + NCOL + 2, :] = jnp.broadcast_to(lg_mid, (1, FR))
    decd[...] = jnp.ones_like(decd)
    decd[1:17, :] = decay[...]

    def prepare(c, d, present, block):
        ld = jnp.log1p(d - 1.0)
        gain = jnp.sqrt(1.0 - d * d) * present
        lc = t_centred * ld + lgb[...]
        f = jnp.exp(lc)
        a = gain * jnp.exp(-lc)
        fwd[:, lanes(c)] = f
        inv[:, lanes(c)] = a
        hi, lo = split_rows(a * a)
        s2 = jnp.dot(tri_lo[...], jnp.concatenate([hi, lo], axis=0), preferred_element_type=F32)
        sq[:, lanes(c)] = s2
        msg_a0[pl.ds(ROWS + c, 1), :] = s2[FR - 1 : FR, :]
        s = block.T
        cur[:, lanes(c)] = s
        x = a * s
        msg_a0[pl.ds(c, 1), :] = jnp.sum(x, axis=0, keepdims=True)
        hi, lo = split_rows(x)
        xh[0:FR, lanes(c)] = hi
        xh[FR : 2 * FR, lanes(c)] = lo

    load_spk.wait()

    def own_column(k, _):
        prepare(k + 1, decd[pl.ds(k + 1, 1), :], 1.0, spk_raw[pl.ds(pl.multiple_of(k * FR, FR), FR), :])
        return 0

    lax.fori_loop(0, 16, own_column, 0)

    pl.semaphore_wait(barrier, len(group) + 2)

    def remote(src, dst, k, device):
        return pltpu.make_async_remote_copy(
            src_ref=src, dst_ref=dst, send_sem=ss.at[k], recv_sem=rs.at[k],
            device_id=device, device_id_type=MESH,
        )

    halo = [
        remote(spk_hbm.at[pl.ds(NEU - FR, FR), :], halo_spk.at[0], 0, upper),
        remote(spk_hbm.at[pl.ds(0, FR), :], halo_spk.at[1], 1, lower),
        remote(decay.at[pl.ds(8, 8), :], halo_dec.at[0], 2, upper),
        remote(decay.at[pl.ds(0, 8), :], halo_dec.at[1], 3, lower),
    ]
    for copy in halo:
        copy.start()

    def names(q, k, v):
        return jnp.where(pat[q, k] - q == v, 1.0, 0.0)

    def sources(q):
        own = [[names(q, k, v) for k in range(K)] for v in (0, 2, 4)]
        return own + [[1.0 - own[0][k] - own[1][k] - own[2][k] for k in range(K)]]

    def is_one(q):
        return sum(names(q, k, 1) for k in range(K))

    load_foot.wait()

    def arrange(q, _):
        at = pl.ds(pl.multiple_of(q * PIX_BLOCK, PIX_BLOCK), PIX_BLOCK)
        turned = foot_raw[at, :].T
        chunks = [turned[k * NEU_BLOCK : (k + 1) * NEU_BLOCK, :] for k in range(K)]
        for s, weights in enumerate(sources(q)):
            mixed = sum(chunks[k] * jnp.full((1, PIX_BLOCK), weights[k], F32).astype(BF16) for k in range(K))
            fpt[q, s * NEU_BLOCK : (s + 1) * NEU_BLOCK, :] = mixed
        fp[q] = fpt[q].T
        return 0

    lax.fori_loop(0, 32, arrange, 0)

    for copy in halo:
        copy.wait_recv()
    decd[0:1, :] = halo_dec[0, 7:8, :]
    decd[17:18, :] = halo_dec[1, 0:1, :]
    has_lower = jnp.where(tile > 0, 1.0, 0.0)
    has_upper = jnp.where(tile < NTILE - 1, 1.0, 0.0)
    prepare(0, decd[0:1, :], has_lower, halo_spk[0])
    prepare(17, decd[17:18, :], has_upper, halo_spk[1])

    def group_send(src, got, k):
        for r in range(1, NT):
            remote(src, got.at[r - 1], k, (lax.rem(tm + r, NT), tile)).start()
        got[NT - 1] = src[...]

    def group_wait(got, k):
        part = got.at[pl.ds(0, NT - 1)]
        remote(part, part, k, upper).wait_recv()

    def group_sent(got, k):
        part = got.at[pl.ds(0, NT - 1)]
        remote(part, part, k, upper).wait_send()

    def slot_of(j):
        return lax.rem(tm - j + NT - 1, NT)

    def cumulate(tri, out):
        def body(c, _):
            at = lanes(c, 256)
            out[:, at] = jnp.dot(tri[...], xh[:, at], preferred_element_type=F32)
            return 0

        lax.fori_loop(0, NCOL // 2, body, 0)

    def put_columns(value):
        def body(c, before):
            y = value(c)
            val_n[:, lanes(c)] = y.astype(BF16)
            turned = pltpu.roll(y, NEU_BLOCK, 1)
            val_s[:, lanes(c)] = jnp.where(low_half, before, turned).astype(BF16)
            return turned

        last = lax.fori_loop(0, NCOL, body, jnp.zeros((FR, FR), F32))
        val_s[:, NCOL * FR : (NCOL + 1) * FR] = last.astype(BF16)

    low_row = lax.broadcasted_iota(jnp.int32, (1, FR), 1) < NEU_BLOCK
    m_lo = jnp.where(low_row, 1.0, 0.0).astype(BF16)
    m_hi = jnp.where(low_row, 0.0, 1.0).astype(BF16)

    def pick(i):
        n0, n1, n2 = (val_n[:, lanes(i + k)] for k in range(3))
        s0, s1, s2 = (val_s[:, lanes(i + 1 + k)] for k in range(3))
        one_e, one_o = is_one(2 * i), is_one(2 * i + 1)

        def pair(x0, x1, x2, y, one):
            a = x0 * m_lo + y * m_hi
            first = jnp.where(low_row, 0.0, one).astype(BF16)
            second = jnp.where(low_row, 0.0, 1.0 - one).astype(BF16)
            b = x2 * m_lo + x0 * first + x1 * second
            return jnp.concatenate([a, b], axis=1)

        return pair(n0, n1, n2, s0, one_e), pair(s0, s1, s2, n1, one_o), one_e, one_o

    def model(i):
        even, odd, one_e, one_o = pick(i)
        y_e = jnp.dot(even, fpt[2 * i], preferred_element_type=F32)
        y_o = jnp.dot(odd, fpt[2 * i + 1], preferred_element_type=F32)
        return y_e, y_o, one_e, one_o

    def residual_step(i):
        y_e, y_o, one_e, one_o = model(i)
        r_e = (y_e - rec_t[2 * i].astype(F32)).astype(BF16)
        r_o = (y_o - rec_t[2 * i + 1].astype(F32)).astype(BF16)
        c = jnp.dot(r_e, fp[2 * i], preferred_element_type=F32)
        d = jnp.dot(r_o, fp[2 * i + 1], preferred_element_type=F32)
        ca, cb, da, db = c[:, :FR], c[:, FR:], d[:, :FR], d[:, FR:]
        acc_n[:, lanes(i)] += jnp.where(low_half, ca, cb * one_e)
        acc_s[:, lanes(i)] += jnp.where(low_half, da, ca + db * one_o)
        acc_n[:, lanes(i + 1)] += jnp.where(low_half, 0.0, cb * (1.0 - one_e) + da)
        acc_s[:, lanes(i + 1)] += jnp.where(low_half, 0.0, db * (1.0 - one_o))
        acc_n[:, lanes(i + 2)] += jnp.where(low_half, cb, 0.0)
        acc_s[:, lanes(i + 2)] += jnp.where(low_half, db, 0.0)

    def total_column(c, first=False):
        before = 0.0 if first else acc_s[:, lanes(c - 1)]
        return acc_n[:, lanes(c)] + pltpu.roll(jnp.where(low_half, acc_s[:, lanes(c)], before), NEU_BLOCK, 1)

    step = None
    for it in range(ITERS):
        msg_a, got_a, sem_a = (msg_a0, got_a0, 4) if it == 0 else (msg_a1, got_a1, 5)
        if it > 0:

            def update(c, _):
                at = lanes(c, 256)
                new = jnp.maximum(cur[:, at] - step * grad[:, at], 0.0)
                cur[:, at] = new
                x = inv[:, at] * new
                sums = jnp.sum(x, axis=0, keepdims=True)
                msg_a1[pl.ds(2 * c, 1), :] = sums[:, :FR]
                msg_a1[pl.ds(2 * c + 1, 1), :] = sums[:, FR:]
                hi, lo = split_rows(x)
                xh[0:FR, at] = hi
                xh[FR : 2 * FR, at] = lo
                return 0

            lax.fori_loop(0, NCOL // 2, update, 0)
        group_send(msg_a, got_a, sem_a)
        cumulate(tri_lo, loc)
        acc_n[...] = jnp.zeros_like(acc_n)
        acc_s[...] = jnp.zeros_like(acc_s)
        if it == 0:
            load_rec.wait()

            def turn(q, _):
                rec_t[q] = rec_raw[pl.ds(pl.multiple_of(q * PIX_BLOCK, PIX_BLOCK), PIX_BLOCK), :].T
                return 0

            lax.fori_loop(0, 32, turn, 0)
        group_wait(got_a, sem_a)
        if it == 0:
            ld = jnp.log1p(decd[...] - 1.0)
            run = None
            for j in range(NT):
                tab = got_a0.at[slot_of(j)]
                tot = tab[ROWS + NCOL : ROWS + NCOL + 1, :]
                mid = tab[ROWS + NCOL + 1 : ROWS + NCOL + 2, :]
                tab_u[j] = jnp.exp(64.0 * ld + (tot - mid))
                tab_e[j] = jnp.exp(64.0 * ld + mid)
                tab_t[j] = jnp.exp(128.0 * ld + tot)
                tab_q[j] = tab_u[j] * tab[ROWS : 2 * ROWS, :]
            run = tab_e[tm]
            for j in range(NT - 1, -1, -1):
                active = j < tm
                tab_c[j] = jnp.where(active, run * tab_u[j], 0.0)
                run = jnp.where(active, run * tab_t[j], run)
        carry = jnp.zeros((ROWS, FR), F32)
        for j in range(NT):
            carry = carry + tab_c[j] * got_a[slot_of(j), 0:ROWS, :]
        row_c[...] = carry

        def traces_of(c):
            y = fwd[:, lanes(c)] * (loc[:, lanes(c)] + row_c[pl.ds(c, 1), :])
            if it == ITERS - 1:
                loc[:, lanes(c)] = y
            return y

        put_columns(traces_of)

        def edge_blocks(k, _):
            residual_step(k + 12 * lax.div(k, 2))
            return 0

        lax.fori_loop(0, 4, edge_blocks, 0)
        msg_b[2 * it, :, :FR] = total_column(0, first=True)
        msg_b[2 * it, :, FR:] = total_column(1)
        msg_b[2 * it + 1, :, :FR] = total_column(16)
        msg_b[2 * it + 1, :, FR:] = total_column(17)
        to_low = remote(msg_b.at[2 * it], got_b.at[2 * it], 6 + 2 * it, lower)
        to_up = remote(msg_b.at[2 * it + 1], got_b.at[2 * it + 1], 7 + 2 * it, upper)
        to_low.start()
        to_up.start()

        def inner_blocks(k, _):
            residual_step(k + 2)
            return 0

        lax.fori_loop(0, 12, inner_blocks, 0)

        def back_column(c, s):
            x = fwd[:, lanes(c)] * s
            msg_cd[it, pl.ds(c, 1), :] = jnp.sum(x, axis=0, keepdims=True)
            msg_cd[it, pl.ds(ROWS + c, 1), :] = jnp.sum(x * sq[:, lanes(c)], axis=0, keepdims=True)
            hi, lo = split_rows(x)
            xh[0:FR, lanes(c)] = hi
            xh[FR : 2 * FR, lanes(c)] = lo

        def inner_column(k, _):
            back_column(k + 2, total_column(k + 2))
            return 0

        lax.fori_loop(0, 14, inner_column, 0)
        to_low.wait_recv()
        to_up.wait_recv()
        back_column(0, msg_b[2 * it, :, :FR] + has_lower * got_b[2 * it + 1, :, :FR])
        back_column(1, msg_b[2 * it, :, FR:] + has_lower * got_b[2 * it + 1, :, FR:])
        back_column(16, msg_b[2 * it + 1, :, :FR] + has_upper * got_b[2 * it, :, :FR])
        back_column(17, msg_b[2 * it + 1, :, FR:] + has_upper * got_b[2 * it, :, FR:])
        group_send(msg_cd.at[it], got_cd.at[it], 10 + it)
        cumulate(tri_up, loc2)

        def square_part(c, _):
            at = lanes(c, 256)
            a = inv[:, at]
            hi, lo = split_rows(a * a * loc2[:, at])
            both = jnp.concatenate([hi, lo], axis=0)
            grad[:, at] = jnp.dot(tri_lo[...], both, preferred_element_type=F32)
            return 0

        lax.fori_loop(0, NCOL // 2, square_part, 0)
        group_wait(got_cd.at[it], 10 + it)
        w = jnp.zeros((ROWS, FR), F32)
        mine = w
        carry = w
        for j in range(NT - 1, -1, -1):
            at = slot_of(j)
            mine = jnp.where(tm == j, w, mine)
            carry = carry + tab_c[j] * (got_cd[it, at, ROWS : 2 * ROWS, :] + tab_q[j] * w)
            w = tab_e[j] * got_cd[it, at, 0:ROWS, :] + tab_t[j] * w
        row_w[...] = tab_u[tm] * mine
        row_c[...] = carry

        def direction_of(c):
            at = lanes(c)
            return fwd[:, at] * (grad[:, at] + sq[:, at] * row_w[pl.ds(c, 1), :] + row_c[pl.ds(c, 1), :])

        put_columns(direction_of)

        def gradient_column(c):
            at = lanes(c)
            g = inv[:, at] * (loc2[:, at] + row_w[pl.ds(c, 1), :])
            grad[:, at] = g
            return g

        def image_step(i, sums):
            g_sum, p_sum = sums
            y_e, y_o, _, _ = model(i)
            p = y_e * y_e + y_o * y_o
            p_sum = p_sum + jnp.sum(p.reshape(16, 8, 256), axis=0)
            g = gradient_column(i + 1)
            g_sum = g_sum + jnp.sum((g * g).reshape(16, 8, FR), axis=0)
            return g_sum, p_sum

        g_sum, p_sum = lax.fori_loop(
            0, 16, image_step, (jnp.zeros((8, FR), F32), jnp.zeros((8, 2 * FR), F32))
        )
        g_row = jnp.sum(g_sum, axis=0, keepdims=True)
        p_row = jnp.sum(p_sum[:, :FR] + p_sum[:, FR:], axis=0, keepdims=True)
        total = jnp.where(
            low_row, g_row + pltpu.roll(g_row, NEU_BLOCK, 1), p_row + pltpu.roll(p_row, NEU_BLOCK, 1)
        )
        for k, (stage, got_e) in enumerate(zip(STAGES, (got_e0, got_e1))):
            msg_e[2 * it + k] = total
            n = len(stage)
            for i, o in enumerate(stage):
                remote(msg_e.at[2 * it + k], got_e.at[it, i], 12 + 2 * it + k, device_at(o)).start()
            if k == 0:
                if it < ITERS - 1:
                    gradient_column(0)
                    gradient_column(17)
            elif it == ITERS - 1:

                def turn_out(c, _):
                    at = lanes(c + 1)
                    to = pl.ds(pl.multiple_of(c * FR, FR), FR)
                    out_tr[to, :] = loc[:, at].T
                    spk_raw[to, :] = cur[:, at].T
                    rec32 = grad[:, at].T
                    out_spk[to, :] = rec32
                    return 0

                lax.fori_loop(0, 16, turn_out, 0)
            everything = got_e.at[it]
            remote(everything, everything, 12 + 2 * it + k, upper).wait_recv()
            parts = [total] + [got_e[it, i] for i in range(n)]
            while len(parts) > 1:
                parts = [a + b for a, b in zip(parts[::2], parts[1::2])] + parts[len(parts) // 2 * 2 :]
            total = parts[0]
        grad_sq = jnp.sum(jnp.where(low_row, total, 0.0), axis=1, keepdims=True)
        image_sq = jnp.sum(jnp.where(low_row, 0.0, total), axis=1, keepdims=True)
        step = grad_sq / (image_sq + 1e-06)

    def finish(c, _):
        to = pl.ds(pl.multiple_of(c * 256, 256), 256)
        out_spk[to, :] = jnp.maximum(spk_raw[to, :] - step * out_spk[to, :], 0.0)
        return 0

    lax.fori_loop(0, 8, finish, 0)

    for copy in halo:
        copy.wait_send()
    group_sent(got_a0, 4)
    group_sent(got_a1, 5)
    for it in range(ITERS):
        remote(msg_b.at[2 * it], got_b.at[2 * it], 6 + 2 * it, lower).wait_send()
        remote(msg_b.at[2 * it + 1], got_b.at[2 * it + 1], 7 + 2 * it, upper).wait_send()
        group_sent(got_cd.at[it], 10 + it)
        for k, got_e in enumerate((got_e0, got_e1)):
            everything = got_e.at[it]
            remote(everything, everything, 12 + 2 * it + k, upper).wait_send()


def per_device(recording, footprints, pattern, decay, frame_gain, spikes):
    wide = (FR, NCOL * FR)
    vm = pltpu.VMEM
    scratch = [
        vm((PIX, 256), BF16), vm((PIX, FR), BF16), vm((NEU, FR), F32),
        vm((32, 256, 256), BF16), vm((32, 256, 256), BF16), vm((32, FR, 256), BF16),
        vm(wide, F32), vm(wide, F32), vm(wide, F32), vm(wide, F32), vm(wide, F32),
        vm((2 * FR, NCOL * FR), BF16), vm(wide, F32), vm(wide, F32), vm(wide, F32), vm(wide, F32),
        vm(wide, BF16), vm((FR, (NCOL + 1) * FR), BF16),
        vm((FR, FR), F32), vm((FR, 2 * FR), BF16), vm((FR, 2 * FR), BF16),
        vm((ROWS, FR), F32),
        vm((NT, ROWS, FR), F32), vm((NT, ROWS, FR), F32), vm((NT, ROWS, FR), F32),
        vm((NT, ROWS, FR), F32), vm((NT, ROWS, FR), F32),
        vm((ROWS, FR), F32), vm((ROWS, FR), F32),
        vm((2, FR, FR), F32), vm((2, 8, FR), F32),
        vm((2 * ROWS, FR), F32), vm((ROWS, FR), F32), vm((ITERS, 2 * ROWS, FR), F32),
        vm((NT, 2 * ROWS, FR), F32), vm((NT, ROWS, FR), F32), vm((ITERS, NT, 2 * ROWS, FR), F32),
        vm((2 * ITERS, FR, 2 * FR), F32), vm((2 * ITERS, FR, 2 * FR), F32),
        vm((2 * ITERS, 1, FR), F32),
        vm((ITERS, len(STAGES[0]), 1, FR), F32), vm((ITERS, len(STAGES[1]), 1, FR), F32),
        pltpu.SemaphoreType.DMA((16,)), pltpu.SemaphoreType.DMA((16,)), pltpu.SemaphoreType.DMA((3,)),
    ]
    anywhere = pl.BlockSpec(memory_space=pl.ANY)
    in_vmem = pl.BlockSpec(memory_space=pltpu.VMEM)
    return pl.pallas_call(
        kernel,
        out_shape=(jax.ShapeDtypeStruct((NEU, FR), F32), jax.ShapeDtypeStruct((NEU, FR), F32)),
        in_specs=[
            anywhere, anywhere, pl.BlockSpec(memory_space=pltpu.SMEM), in_vmem, in_vmem, anywhere,
        ],
        out_specs=(in_vmem, in_vmem),
        scratch_shapes=scratch,
        compiler_params=pltpu.CompilerParams(
            collective_id=0, has_side_effects=True, vmem_limit_bytes=60 * 2**20
        ),
        name="deconvolve",
    )(
        recording, footprints, pattern, decay.reshape(16, FR), frame_gain.reshape(1, FR), spikes,
    )


def solution(mesh):
    return jax.shard_map(
        per_device,
        mesh=mesh,
        in_specs=(
            P("tile", "tm"),
            P("tile", None),
            P("tile", None),
            P("tile"),
            P("tm"),
            P("tile", "tm"),
        ),
        out_specs=(P("tile", "tm"), P("tile", "tm")),
        check_vma=False,
    )
```

```python
import functools
import itertools

import jax
import jax.numpy as jnp
from jax import lax
from jax.experimental import pallas as pl
from jax.experimental.pallas import tpu as pltpu
from jax.sharding import PartitionSpec as P

NEU_BLOCK = 64
PIX_BLOCK = 256
K = 4
HB = 2
ITERS = 2

NX, NY, NZ, NC = 4, 4, 8, 2
NT = NX * NC
NTILE = NY * NZ
FR = 128
NCOL = 18
ROWS = 24
NEU = 2048
PIX = 8192
MESH = pl.DeviceIdType.MESH
F32 = jnp.float32
BF16 = jnp.bfloat16


def ring_distance(d, n):
    return min(d, n - d)


def offsets(keep):
    found = []
    for dx, dy, dz, dc in itertools.product(range(NX), range(NY), range(NZ), range(NC)):
        if (dx, dy, dz, dc) != (0, 0, 0, 0) and keep(dx, dy, dz, dc):
            far = ring_distance(dx, NX) + ring_distance(dy, NY) + ring_distance(dz, NZ)
            found.append((-far, dx, dy, dz, dc))
    return [o[1:] for o in sorted(found)]


TM_GROUP = offsets(lambda dx, dy, dz, dc: dy == 0 and dz == 0)
CORE_GROUP = offsets(lambda dx, dy, dz, dc: dx == 0 and dy == 0 and dz == 0)
CHIP_GROUP = offsets(lambda dx, dy, dz, dc: dc == 0)
STAGES = (CORE_GROUP, CHIP_GROUP)


def split_rows(x):
    hi = x.astype(BF16)
    lo = (x - hi.astype(F32)).astype(BF16)
    return hi, lo


def kernel(
    rec_hbm, foot_hbm, pat_hbm, dec_hbm, gain_hbm, spk_hbm,
    out_spk, out_tr,
    foot_raw, rec_raw, spk_raw, decay, fgain, pat, fp, fpt, rec_t,
    cur, grad, fwd, inv, sq, xh, loc, loc2, acc_n, acc_s, val_n, val_s,
    lgb, tri_lo, tri_up, decd, tab_u, tab_e, tab_t, tab_q, tab_c, row_w, row_c,
    halo_spk, halo_dec, msg_a0, msg_a1, msg_cd, got_a0, got_a1, got_cd,
    msg_b, got_b, msg_e, got_e0, got_e1,
    ss, rs, ls,
):
    tm = lax.axis_index("tm")
    tile = lax.axis_index("tile")
    px, pc = lax.div(tm, NC), lax.rem(tm, NC)
    py, pz = lax.div(tile, NZ), lax.rem(tile, NZ)

    def device_at(o):
        dx, dy, dz, dc = o
        x = lax.rem(px + dx, NX) if dx else px
        c = lax.rem(pc + dc, NC) if dc else pc
        y = lax.rem(py + dy, NY) if dy else py
        z = lax.rem(pz + dz, NZ) if dz else pz
        return (x * NC + c, y * NZ + z)

    upper = (tm, lax.rem(tile + 1, NTILE))
    lower = (tm, lax.rem(tile + NTILE - 1, NTILE))

    group = offsets(lambda *o: o in TM_GROUP or o in CORE_GROUP or o in CHIP_GROUP)
    barrier = pltpu.get_barrier_semaphore()
    for o in group:
        pl.semaphore_signal(barrier, inc=1, device_id=device_at(o), device_id_type=MESH)
    for d in (upper, lower):
        pl.semaphore_signal(barrier, inc=1, device_id=d, device_id_type=MESH)

    load_dec = pltpu.make_async_copy(dec_hbm, decay, ls.at[3])
    load_gain = pltpu.make_async_copy(gain_hbm, fgain, ls.at[4])
    load_pat = pltpu.make_async_copy(pat_hbm, pat, ls.at[5])
    load_spk = pltpu.make_async_copy(spk_hbm, spk_raw, ls.at[0])
    load_foot = pltpu.make_async_copy(foot_hbm, foot_raw, ls.at[1])
    load_rec = pltpu.make_async_copy(rec_hbm, rec_raw, ls.at[2])
    for load in (load_dec, load_gain, load_pat, load_spk, load_foot, load_rec):
        load.start()

    def lanes(c, width=128):
        return pl.ds(pl.multiple_of(c * width, width), width)

    row = lax.broadcasted_iota(jnp.int32, (FR, FR), 0)
    col = lax.broadcasted_iota(jnp.int32, (FR, FR), 1)
    low_half = col < NEU_BLOCK
    t_centred = (row - 63).astype(F32)

    lower_tri = (row >= col).astype(BF16)
    upper_tri = (row <= col).astype(BF16)
    tri_lo[:, :FR] = lower_tri
    tri_lo[:, FR:] = lower_tri
    tri_up[:, :FR] = upper_tri
    tri_up[:, FR:] = upper_tri

    load_gain.wait()
    log_fg = jnp.log(fgain[...])
    lg = jnp.sum(jnp.where(row >= col, log_fg, 0.0), axis=1, keepdims=True)
    lg_mid = lg[63:64, :]
    lg_tot = lg[127:128, :]
    lgb[...] = jnp.broadcast_to(lg - lg_mid, (FR, FR))

    msg_a0[...] = jnp.zeros_like(msg_a0)
    msg_a1[...] = jnp.zeros_like(msg_a1)
    msg_cd[...] = jnp.zeros_like(msg_cd)
    msg_a0[ROWS + NCOL : ROWS + NCOL + 1, :] = jnp.broadcast_to(lg_tot, (1, FR))
    msg_a0[ROWS + NCOL + 1 : ROWS + NCOL + 2, :] = jnp.broadcast_to(lg_mid, (1, FR))
    decd[...] = jnp.ones_like(decd)
    load_dec.wait()
    decd[1:17, :] = decay[...]

    def prepare(c, d, present, block):
        ld = jnp.log1p(d - 1.0)
        gain = jnp.sqrt(1.0 - d * d) * present
        lc = t_centred * ld + lgb[...]
        f = jnp.exp(lc)
        a = gain * jnp.exp(-lc)
        fwd[:, lanes(c)] = f
        inv[:, lanes(c)] = a
        hi, lo = split_rows(a * a)
        s2 = jnp.dot(tri_lo[...], jnp.concatenate([hi, lo], axis=0), preferred_element_type=F32)
        sq[:, lanes(c)] = s2
        msg_a0[pl.ds(ROWS + c, 1), :] = s2[FR - 1 : FR, :]
        s = block.T
        cur[:, lanes(c)] = s
        x = a * s
        msg_a0[pl.ds(c, 1), :] = jnp.sum(x, axis=0, keepdims=True)
        hi, lo = split_rows(x)
        xh[0:FR, lanes(c)] = hi
        xh[FR : 2 * FR, lanes(c)] = lo

    load_spk.wait()

    def own_column(k, _):
        prepare(k + 1, decd[pl.ds(k + 1, 1), :], 1.0, spk_raw[pl.ds(pl.multiple_of(k * FR, FR), FR), :])
        return 0

    lax.fori_loop(0, 16, own_column, 0, unroll=4)

    def names(q, k, v):
        return jnp.where(pat[k, q] - q == v, 1.0, 0.0)

    def sources(q):
        own = [[names(q, k, v) for k in range(K)] for v in (0, 2, 4)]
        return own + [[1.0 - own[0][k] - own[1][k] - own[2][k] for k in range(K)]]

    def is_one(q):
        return sum(names(q, k, 1) for k in range(K))

    load_pat.wait()
    load_foot.wait()

    def arrange(q, _):
        at = pl.ds(pl.multiple_of(q * PIX_BLOCK, PIX_BLOCK), PIX_BLOCK)
        turned = foot_raw[at, :].T
        chunks = [turned[k * NEU_BLOCK : (k + 1) * NEU_BLOCK, :] for k in range(K)]
        for s, weights in enumerate(sources(q)):
            mixed = sum(chunks[k] * jnp.full((1, PIX_BLOCK), weights[k], F32).astype(BF16) for k in range(K))
            fpt[q, s * NEU_BLOCK : (s + 1) * NEU_BLOCK, :] = mixed
        fp[q] = fpt[q].T
        return 0


    lax.fori_loop(0, 16, arrange, 0, unroll=4)

    pl.semaphore_wait(barrier, len(group) + 2)

    def remote(src, dst, k, device):
        return pltpu.make_async_remote_copy(
            src_ref=src, dst_ref=dst, send_sem=ss.at[k], recv_sem=rs.at[k],
            device_id=device, device_id_type=MESH,
        )

    halo = [
        remote(spk_hbm.at[pl.ds(NEU - FR, FR), :], halo_spk.at[0], 0, upper),
        remote(spk_hbm.at[pl.ds(0, FR), :], halo_spk.at[1], 1, lower),
        remote(decay.at[pl.ds(8, 8), :], halo_dec.at[0], 2, upper),
        remote(decay.at[pl.ds(0, 8), :], halo_dec.at[1], 3, lower),
    ]
    for copy in halo:
        copy.start()

    lax.fori_loop(16, 32, arrange, 0, unroll=4)

    for copy in halo:
        copy.wait_recv()
    decd[0:1, :] = halo_dec[0, 7:8, :]
    decd[17:18, :] = halo_dec[1, 0:1, :]
    has_lower = jnp.where(tile > 0, 1.0, 0.0)
    has_upper = jnp.where(tile < NTILE - 1, 1.0, 0.0)
    prepare(0, decd[0:1, :], has_lower, halo_spk[0])
    prepare(17, decd[17:18, :], has_upper, halo_spk[1])

    def group_send(src, got, k):
        for r in range(1, NT):
            remote(src, got.at[r - 1], k, (lax.rem(tm + r, NT), tile)).start()
        got[NT - 1] = src[...]

    def group_wait(got, k):
        part = got.at[pl.ds(0, NT - 1)]
        remote(part, part, k, upper).wait_recv()

    def group_sent(got, k):
        part = got.at[pl.ds(0, NT - 1)]
        remote(part, part, k, upper).wait_send()

    def slot_of(j):
        return lax.rem(tm - j + NT - 1, NT)

    def cumulate(tri, out):
        def body(c, _):
            at = lanes(c, 256)
            out[:, at] = jnp.dot(tri[...], xh[:, at], preferred_element_type=F32)
            return 0

        lax.fori_loop(0, NCOL // 2, body, 0, unroll=9)

    def put_columns(value):
        def body(c, before):
            y = value(c)
            val_n[:, lanes(c)] = y.astype(BF16)
            turned = pltpu.roll(y, NEU_BLOCK, 1)
            val_s[:, lanes(c)] = jnp.where(low_half, before, turned).astype(BF16)
            return turned

        last = lax.fori_loop(0, NCOL, body, jnp.zeros((FR, FR), F32), unroll=6)
        val_s[:, NCOL * FR : (NCOL + 1) * FR] = last.astype(BF16)

    low_row = lax.broadcasted_iota(jnp.int32, (1, FR), 1) < NEU_BLOCK
    m_lo = jnp.where(low_row, 1.0, 0.0).astype(BF16)
    m_hi = jnp.where(low_row, 0.0, 1.0).astype(BF16)

    def pick(i):
        n0, n1, n2 = (val_n[:, lanes(i + k)] for k in range(3))
        s0, s1, s2 = (val_s[:, lanes(i + 1 + k)] for k in range(3))
        one_e, one_o = is_one(2 * i), is_one(2 * i + 1)

        def pair(x0, x1, x2, y, one):
            a = x0 * m_lo + y * m_hi
            first = jnp.where(low_row, 0.0, one).astype(BF16)
            second = jnp.where(low_row, 0.0, 1.0 - one).astype(BF16)
            b = x2 * m_lo + x0 * first + x1 * second
            return jnp.concatenate([a, b], axis=1)

        return pair(n0, n1, n2, s0, one_e), pair(s0, s1, s2, n1, one_o), one_e, one_o

    def model(i):
        even, odd, one_e, one_o = pick(i)
        y_e = jnp.dot(even, fpt[2 * i], preferred_element_type=F32)
        y_o = jnp.dot(odd, fpt[2 * i + 1], preferred_element_type=F32)
        return y_e, y_o, one_e, one_o

    def residual_step(i):
        y_e, y_o, one_e, one_o = model(i)
        r_e = (y_e - rec_t[2 * i].astype(F32)).astype(BF16)
        r_o = (y_o - rec_t[2 * i + 1].astype(F32)).astype(BF16)
        c = jnp.dot(r_e, fp[2 * i], preferred_element_type=F32)
        d = jnp.dot(r_o, fp[2 * i + 1], preferred_element_type=F32)
        ca, cb, da, db = c[:, :FR], c[:, FR:], d[:, :FR], d[:, FR:]
        acc_n[:, lanes(i)] += jnp.where(low_half, ca, cb * one_e)
        acc_s[:, lanes(i)] += jnp.where(low_half, da, ca + db * one_o)
        acc_n[:, lanes(i + 1)] += jnp.where(low_half, 0.0, cb * (1.0 - one_e) + da)
        acc_s[:, lanes(i + 1)] += jnp.where(low_half, 0.0, db * (1.0 - one_o))
        acc_n[:, lanes(i + 2)] += jnp.where(low_half, cb, 0.0)
        acc_s[:, lanes(i + 2)] += jnp.where(low_half, db, 0.0)

    def total_column(c, first=False):
        before = 0.0 if first else acc_s[:, lanes(c - 1)]
        return acc_n[:, lanes(c)] + pltpu.roll(jnp.where(low_half, acc_s[:, lanes(c)], before), NEU_BLOCK, 1)

    step = None
    for it in range(ITERS):
        msg_a, got_a, sem_a = (msg_a0, got_a0, 4) if it == 0 else (msg_a1, got_a1, 5)
        if it > 0:

            def update(c, _):
                at = lanes(c, 256)
                new = jnp.maximum(cur[:, at] - step * grad[:, at], 0.0)
                cur[:, at] = new
                x = inv[:, at] * new
                sums = jnp.sum(x, axis=0, keepdims=True)
                msg_a1[pl.ds(2 * c, 1), :] = sums[:, :FR]
                msg_a1[pl.ds(2 * c + 1, 1), :] = sums[:, FR:]
                hi, lo = split_rows(x)
                xh[0:FR, at] = hi
                xh[FR : 2 * FR, at] = lo
                return 0

            lax.fori_loop(0, NCOL // 2, update, 0, unroll=3)
        group_send(msg_a, got_a, sem_a)
        cumulate(tri_lo, loc)
        acc_n[...] = jnp.zeros_like(acc_n)
        acc_s[...] = jnp.zeros_like(acc_s)
        if it == 0:
            load_rec.wait()

            def turn(q, _):
                rec_t[q] = rec_raw[pl.ds(pl.multiple_of(q * PIX_BLOCK, PIX_BLOCK), PIX_BLOCK), :].T
                return 0

            lax.fori_loop(0, 32, turn, 0, unroll=8)
        group_wait(got_a, sem_a)
        if it == 0:
            ld = jnp.log1p(decd[...] - 1.0)
            run = None
            for j in range(NT):
                tab = got_a0.at[slot_of(j)]
                tot = tab[ROWS + NCOL : ROWS + NCOL + 1, :]
                mid = tab[ROWS + NCOL + 1 : ROWS + NCOL + 2, :]
                tab_u[j] = jnp.exp(64.0 * ld + (tot - mid))
                tab_e[j] = jnp.exp(64.0 * ld + mid)
                tab_t[j] = jnp.exp(128.0 * ld + tot)
                tab_q[j] = tab_u[j] * tab[ROWS : 2 * ROWS, :]
            run = tab_e[tm]
            for j in range(NT - 1, -1, -1):
                active = j < tm
                tab_c[j] = jnp.where(active, run * tab_u[j], 0.0)
                run = jnp.where(active, run * tab_t[j], run)
        carry = jnp.zeros((ROWS, FR), F32)
        for j in range(NT):
            carry = carry + tab_c[j] * got_a[slot_of(j), 0:ROWS, :]
        row_c[...] = carry

        def traces_of(c):
            y = fwd[:, lanes(c)] * (loc[:, lanes(c)] + row_c[pl.ds(c, 1), :])
            if it == ITERS - 1:
                loc[:, lanes(c)] = y
            return y

        put_columns(traces_of)

        def edge_blocks(k, _):
            residual_step(k + 12 * lax.div(k, 2))
            return 0

        lax.fori_loop(0, 4, edge_blocks, 0, unroll=4)
        msg_b[2 * it, :, :FR] = total_column(0, first=True)
        msg_b[2 * it, :, FR:] = total_column(1)
        msg_b[2 * it + 1, :, :FR] = total_column(16)
        msg_b[2 * it + 1, :, FR:] = total_column(17)
        to_low = remote(msg_b.at[2 * it], got_b.at[2 * it], 6 + 2 * it, lower)
        to_up = remote(msg_b.at[2 * it + 1], got_b.at[2 * it + 1], 7 + 2 * it, upper)
        to_low.start()
        to_up.start()

        def inner_blocks(k, _):
            residual_step(k + 2)
            return 0

        lax.fori_loop(0, 12, inner_blocks, 0, unroll=12)

        def back_column(c, s):
            x = fwd[:, lanes(c)] * s
            msg_cd[it, pl.ds(c, 1), :] = jnp.sum(x, axis=0, keepdims=True)
            msg_cd[it, pl.ds(ROWS + c, 1), :] = jnp.sum(x * sq[:, lanes(c)], axis=0, keepdims=True)
            hi, lo = split_rows(x)
            xh[0:FR, lanes(c)] = hi
            xh[FR : 2 * FR, lanes(c)] = lo

        def inner_column(k, _):
            back_column(k + 2, total_column(k + 2))
            return 0

        lax.fori_loop(0, 14, inner_column, 0, unroll=7)
        to_low.wait_recv()
        to_up.wait_recv()
        back_column(0, msg_b[2 * it, :, :FR] + has_lower * got_b[2 * it + 1, :, :FR])
        back_column(1, msg_b[2 * it, :, FR:] + has_lower * got_b[2 * it + 1, :, FR:])
        back_column(16, msg_b[2 * it + 1, :, :FR] + has_upper * got_b[2 * it, :, :FR])
        back_column(17, msg_b[2 * it + 1, :, FR:] + has_upper * got_b[2 * it, :, FR:])
        group_send(msg_cd.at[it], got_cd.at[it], 10 + it)
        cumulate(tri_up, loc2)

        def square_part(c, _):
            at = lanes(c, 256)
            a = inv[:, at]
            hi, lo = split_rows(a * a * loc2[:, at])
            both = jnp.concatenate([hi, lo], axis=0)
            grad[:, at] = jnp.dot(tri_lo[...], both, preferred_element_type=F32)
            return 0

        lax.fori_loop(0, NCOL // 2, square_part, 0, unroll=9)
        group_wait(got_cd.at[it], 10 + it)
        w = jnp.zeros((ROWS, FR), F32)
        mine = w
        carry = w
        for j in range(NT - 1, -1, -1):
            at = slot_of(j)
            mine = jnp.where(tm == j, w, mine)
            carry = carry + tab_c[j] * (got_cd[it, at, ROWS : 2 * ROWS, :] + tab_q[j] * w)
            w = tab_e[j] * got_cd[it, at, 0:ROWS, :] + tab_t[j] * w
        row_w[...] = tab_u[tm] * mine
        row_c[...] = carry

        def direction_of(c):
            at = lanes(c)
            return fwd[:, at] * (grad[:, at] + sq[:, at] * row_w[pl.ds(c, 1), :] + row_c[pl.ds(c, 1), :])

        put_columns(direction_of)

        def gradient_column(c):
            at = lanes(c)
            g = inv[:, at] * (loc2[:, at] + row_w[pl.ds(c, 1), :])
            grad[:, at] = g
            return g

        def image_step(i, sums):
            g_sum, p_sum = sums
            y_e, y_o, _, _ = model(i)
            p = y_e * y_e + y_o * y_o
            p_sum = p_sum + jnp.sum(p.reshape(16, 8, 256), axis=0)
            g = gradient_column(i + 1)
            g_sum = g_sum + jnp.sum((g * g).reshape(16, 8, FR), axis=0)
            return g_sum, p_sum

        g_sum, p_sum = lax.fori_loop(
            0, 16, image_step, (jnp.zeros((8, FR), F32), jnp.zeros((8, 2 * FR), F32)), unroll=16
        )
        g_row = jnp.sum(g_sum, axis=0, keepdims=True)
        p_row = jnp.sum(p_sum[:, :FR] + p_sum[:, FR:], axis=0, keepdims=True)
        total = jnp.where(
            low_row, g_row + pltpu.roll(g_row, NEU_BLOCK, 1), p_row + pltpu.roll(p_row, NEU_BLOCK, 1)
        )
        for k, (stage, got_e) in enumerate(zip(STAGES, (got_e0, got_e1))):
            msg_e[2 * it + k] = total
            n = len(stage)
            for i, o in enumerate(stage):
                remote(msg_e.at[2 * it + k], got_e.at[it, i], 12 + 2 * it + k, device_at(o)).start()
            if k == 0:
                if it < ITERS - 1:
                    gradient_column(0)
                    gradient_column(17)
            elif it == ITERS - 1:

                def turn_out(c, _):
                    at = lanes(c + 1)
                    to = pl.ds(pl.multiple_of(c * FR, FR), FR)
                    out_tr[to, :] = loc[:, at].T
                    spk_raw[to, :] = cur[:, at].T
                    rec32 = grad[:, at].T
                    out_spk[to, :] = rec32
                    return 0

                lax.fori_loop(0, 16, turn_out, 0, unroll=4)
            everything = got_e.at[it]
            remote(everything, everything, 12 + 2 * it + k, upper).wait_recv()
            parts = [total] + [got_e[it, i] for i in range(n)]
            while len(parts) > 1:
                parts = [a + b for a, b in zip(parts[::2], parts[1::2])] + parts[len(parts) // 2 * 2 :]
            total = parts[0]
        grad_sq = jnp.sum(jnp.where(low_row, total, 0.0), axis=1, keepdims=True)
        image_sq = jnp.sum(jnp.where(low_row, 0.0, total), axis=1, keepdims=True)
        step = grad_sq / (image_sq + 1e-06)

    def finish(c, _):
        to = pl.ds(pl.multiple_of(c * 256, 256), 256)
        out_spk[to, :] = jnp.maximum(spk_raw[to, :] - step * out_spk[to, :], 0.0)
        return 0

    lax.fori_loop(0, 8, finish, 0, unroll=4)

    for copy in halo:
        copy.wait_send()
    group_sent(got_a0, 4)
    group_sent(got_a1, 5)
    for it in range(ITERS):
        remote(msg_b.at[2 * it], got_b.at[2 * it], 6 + 2 * it, lower).wait_send()
        remote(msg_b.at[2 * it + 1], got_b.at[2 * it + 1], 7 + 2 * it, upper).wait_send()
        group_sent(got_cd.at[it], 10 + it)
        for k, got_e in enumerate((got_e0, got_e1)):
            everything = got_e.at[it]
            remote(everything, everything, 12 + 2 * it + k, upper).wait_send()


def per_device(recording, footprints, pattern, decay, frame_gain, spikes):
    wide = (FR, NCOL * FR)
    vm = pltpu.VMEM
    scratch = [
        vm((PIX, 256), BF16), vm((PIX, FR), BF16), vm((NEU, FR), F32),
        vm((16, FR), F32), vm((1, FR), F32), pltpu.SMEM((K, 32), jnp.int32),
        vm((32, 256, 256), BF16), vm((32, 256, 256), BF16), vm((32, FR, 256), BF16),
        vm(wide, F32), vm(wide, F32), vm(wide, F32), vm(wide, F32), vm(wide, F32),
        vm((2 * FR, NCOL * FR), BF16), vm(wide, F32), vm(wide, F32), vm(wide, F32), vm(wide, F32),
        vm(wide, BF16), vm((FR, (NCOL + 1) * FR), BF16),
        vm((FR, FR), F32), vm((FR, 2 * FR), BF16), vm((FR, 2 * FR), BF16),
        vm((ROWS, FR), F32),
        vm((NT, ROWS, FR), F32), vm((NT, ROWS, FR), F32), vm((NT, ROWS, FR), F32),
        vm((NT, ROWS, FR), F32), vm((NT, ROWS, FR), F32),
        vm((ROWS, FR), F32), vm((ROWS, FR), F32),
        vm((2, FR, FR), F32), vm((2, 8, FR), F32),
        vm((2 * ROWS, FR), F32), vm((ROWS, FR), F32), vm((ITERS, 2 * ROWS, FR), F32),
        vm((NT, 2 * ROWS, FR), F32), vm((NT, ROWS, FR), F32), vm((ITERS, NT, 2 * ROWS, FR), F32),
        vm((2 * ITERS, FR, 2 * FR), F32), vm((2 * ITERS, FR, 2 * FR), F32),
        vm((2 * ITERS, 1, FR), F32),
        vm((ITERS, len(STAGES[0]), 1, FR), F32), vm((ITERS, len(STAGES[1]), 1, FR), F32),
        pltpu.SemaphoreType.DMA((16,)), pltpu.SemaphoreType.DMA((16,)), pltpu.SemaphoreType.DMA((6,)),
    ]
    anywhere = pl.BlockSpec(memory_space=pl.ANY)
    in_vmem = pl.BlockSpec(memory_space=pltpu.VMEM)
    return pl.pallas_call(
        kernel,
        out_shape=(pltpu.VMEM((NEU, FR), F32), pltpu.VMEM((NEU, FR), F32)),
        in_specs=[
            anywhere, anywhere, anywhere, anywhere, anywhere, anywhere,
        ],
        out_specs=(in_vmem, in_vmem),
        scratch_shapes=scratch,
        compiler_params=pltpu.CompilerParams(
            collective_id=0, has_side_effects=True, vmem_limit_bytes=60 * 2**20
        ),
        name="deconvolve",
    )(
        recording, footprints, pattern.T, decay.reshape(16, FR), frame_gain.reshape(1, FR), spikes,
    )


def solution(mesh):
    return jax.shard_map(
        per_device,
        mesh=mesh,
        in_specs=(
            P("tile", "tm"),
            P("tile", None),
            P("tile", None),
            P("tile"),
            P("tm"),
            P("tile", "tm"),
        ),
        out_specs=(P("tile", "tm"), P("tile", "tm")),
        check_vma=False,
    )
```

```python
import functools
import itertools

import jax
import jax.numpy as jnp
from jax import lax
from jax.experimental import pallas as pl
from jax.experimental.pallas import tpu as pltpu
from jax.sharding import PartitionSpec as P

NEU_BLOCK = 64
PIX_BLOCK = 256
K = 4
HB = 2
ITERS = 2

NX, NY, NZ, NC = 4, 4, 8, 2
NT = NX * NC
NTILE = NY * NZ
FR = 128
NCOL = 18
ROWS = 24
NEU = 2048
PIX = 8192
MESH = pl.DeviceIdType.MESH
F32 = jnp.float32
BF16 = jnp.bfloat16


def ring_distance(d, n):
    return min(d, n - d)


def offsets(keep):
    found = []
    for dx, dy, dz, dc in itertools.product(range(NX), range(NY), range(NZ), range(NC)):
        if (dx, dy, dz, dc) != (0, 0, 0, 0) and keep(dx, dy, dz, dc):
            far = ring_distance(dx, NX) + ring_distance(dy, NY) + ring_distance(dz, NZ)
            found.append((-far, dx, dy, dz, dc))
    return [o[1:] for o in sorted(found)]


TM_GROUP = offsets(lambda dx, dy, dz, dc: dy == 0 and dz == 0)
CORE_GROUP = offsets(lambda dx, dy, dz, dc: dx == 0 and dy == 0 and dz == 0)
CHIP_GROUP = offsets(lambda dx, dy, dz, dc: dc == 0)
STAGES = (CORE_GROUP, CHIP_GROUP)


def split_rows(x):
    hi = x.astype(BF16)
    lo = (x - hi.astype(F32)).astype(BF16)
    return hi, lo


def kernel(
    rec_hbm, foot_hbm, pat_hbm, dec_hbm, gain_hbm, spk_hbm,
    out_spk, out_tr,
    foot_raw, rec_raw, spk_raw, decay, fgain, pat, fp, fpt, rec_t,
    cur, grad, fwd, inv, sq, xh, loc, loc2, acc_n, acc_s, val_n, val_s,
    lgb, tri_lo, tri_up, decd, tab_u, tab_e, tab_t, tab_q, tab_c, row_w, row_c,
    halo_spk, halo_dec, msg_a0, msg_a1, msg_cd, got_a0, got_a1, got_cd,
    msg_b, got_b, msg_h, got_h, msg_e, got_e0, got_e1,
    ss, rs, ls,
):
    tm = lax.axis_index("tm")
    tile = lax.axis_index("tile")
    px, pc = lax.div(tm, NC), lax.rem(tm, NC)
    py, pz = lax.div(tile, NZ), lax.rem(tile, NZ)

    def device_at(o):
        dx, dy, dz, dc = o
        x = lax.rem(px + dx, NX) if dx else px
        c = lax.rem(pc + dc, NC) if dc else pc
        y = lax.rem(py + dy, NY) if dy else py
        z = lax.rem(pz + dz, NZ) if dz else pz
        return (x * NC + c, y * NZ + z)

    upper = (tm, lax.rem(tile + 1, NTILE))
    lower = (tm, lax.rem(tile + NTILE - 1, NTILE))

    group = offsets(lambda *o: o in TM_GROUP or o in CORE_GROUP or o in CHIP_GROUP)
    sides = ((0, 1), (1, NTILE - 1))
    crossed = [(lax.rem(tm + k, NT), lax.rem(tile + by, NTILE)) for _, by in sides for k in range(1, NT, 2)]
    barrier = pltpu.get_barrier_semaphore()
    for o in group:
        pl.semaphore_signal(barrier, inc=1, device_id=device_at(o), device_id_type=MESH)
    for d in crossed:
        pl.semaphore_signal(barrier, inc=1, device_id=d, device_id_type=MESH)

    load_dec = pltpu.make_async_copy(dec_hbm, decay, ls.at[3])
    load_gain = pltpu.make_async_copy(gain_hbm, fgain, ls.at[4])
    load_pat = pltpu.make_async_copy(pat_hbm, pat, ls.at[5])
    load_spk = pltpu.make_async_copy(spk_hbm, spk_raw, ls.at[0])
    load_foot = pltpu.make_async_copy(foot_hbm, foot_raw, ls.at[1])
    load_rec = pltpu.make_async_copy(rec_hbm, rec_raw, ls.at[2])
    for load in (load_dec, load_gain, load_pat, load_spk, load_foot, load_rec):
        load.start()

    def lanes(c, width=128):
        return pl.ds(pl.multiple_of(c * width, width), width)

    row = lax.broadcasted_iota(jnp.int32, (FR, FR), 0)
    col = lax.broadcasted_iota(jnp.int32, (FR, FR), 1)
    low_half = col < NEU_BLOCK
    t_centred = (row - 63).astype(F32)

    lower_tri = (row >= col).astype(BF16)
    upper_tri = (row <= col).astype(BF16)
    tri_lo[:, :FR] = lower_tri
    tri_lo[:, FR:] = lower_tri
    tri_up[:, :FR] = upper_tri
    tri_up[:, FR:] = upper_tri

    load_gain.wait()
    log_fg = jnp.log(fgain[...])
    lg = jnp.sum(jnp.where(row >= col, log_fg, 0.0), axis=1, keepdims=True)
    lg_mid = lg[63:64, :]
    lg_tot = lg[127:128, :]
    lgb[...] = jnp.broadcast_to(lg - lg_mid, (FR, FR))

    msg_a0[...] = jnp.zeros_like(msg_a0)
    msg_a1[...] = jnp.zeros_like(msg_a1)
    msg_cd[...] = jnp.zeros_like(msg_cd)
    msg_a0[ROWS + NCOL : ROWS + NCOL + 1, :] = jnp.broadcast_to(lg_tot, (1, FR))
    msg_a0[ROWS + NCOL + 1 : ROWS + NCOL + 2, :] = jnp.broadcast_to(lg_mid, (1, FR))
    decd[...] = jnp.ones_like(decd)
    load_dec.wait()
    decd[1:17, :] = decay[...]

    def prepare(c, d, present, block, own):
        ld = jnp.log1p(d - 1.0)
        gain = jnp.sqrt(1.0 - d * d) * present
        lc = t_centred * ld + lgb[...]
        f = jnp.exp(lc)
        a = gain * jnp.exp(-lc)
        fwd[:, lanes(c)] = f
        inv[:, lanes(c)] = a
        hi, lo = split_rows(a * a)
        s2 = jnp.dot(tri_lo[...], jnp.concatenate([hi, lo], axis=0), preferred_element_type=F32)
        sq[:, lanes(c)] = s2
        if own:
            msg_a0[pl.ds(ROWS + c, 1), :] = s2[FR - 1 : FR, :]
        s = block.T
        cur[:, lanes(c)] = s
        x = a * s
        if own:
            msg_a0[pl.ds(c, 1), :] = jnp.sum(x, axis=0, keepdims=True)
        hi, lo = split_rows(x)
        xh[0:FR, lanes(c)] = hi
        xh[FR : 2 * FR, lanes(c)] = lo

    load_spk.wait()

    def own_column(k, _):
        prepare(k + 1, decd[pl.ds(k + 1, 1), :], 1.0, spk_raw[pl.ds(pl.multiple_of(k * FR, FR), FR), :], True)
        return 0

    lax.fori_loop(0, 16, own_column, 0, unroll=4)

    def names(q, k, v):
        return jnp.where(pat[k, q] - q == v, 1.0, 0.0)

    def sources(q):
        own = [[names(q, k, v) for k in range(K)] for v in (0, 2, 4)]
        return own + [[1.0 - own[0][k] - own[1][k] - own[2][k] for k in range(K)]]

    def is_one(q):
        return sum(names(q, k, 1) for k in range(K))

    load_pat.wait()
    load_foot.wait()

    def arrange(q, _):
        at = pl.ds(pl.multiple_of(q * PIX_BLOCK, PIX_BLOCK), PIX_BLOCK)
        turned = foot_raw[at, :].T
        chunks = [turned[k * NEU_BLOCK : (k + 1) * NEU_BLOCK, :] for k in range(K)]
        for s, weights in enumerate(sources(q)):
            mixed = sum(chunks[k] * jnp.full((1, PIX_BLOCK), weights[k], F32).astype(BF16) for k in range(K))
            fpt[q, s * NEU_BLOCK : (s + 1) * NEU_BLOCK, :] = mixed
        fp[q] = fpt[q].T
        return 0


    lax.fori_loop(0, 16, arrange, 0, unroll=4)

    pl.semaphore_wait(barrier, len(group) + len(crossed))

    def remote(src, dst, k, device):
        return pltpu.make_async_remote_copy(
            src_ref=src, dst_ref=dst, send_sem=ss.at[k], recv_sem=rs.at[k],
            device_id=device, device_id_type=MESH,
        )

    def group_send(src, got, k):
        for r in range(1, NT):
            remote(src, got.at[r - 1], k, (lax.rem(tm + r, NT), tile)).start()
        got[NT - 1] = src[...]

    def group_wait(got, k):
        part = got.at[pl.ds(0, NT - 1)]
        remote(part, part, k, upper).wait_recv()

    def group_sent(got, k):
        part = got.at[pl.ds(0, NT - 1)]
        remote(part, part, k, upper).wait_send()

    def slot_of(j):
        return lax.rem(tm - j + NT - 1, NT)

    def wide_send(src, got, k):
        for side, by in sides:
            for r in range(NT):
                to = (lax.rem(tm + r, NT), lax.rem(tile + by, NTILE))
                remote(src.at[side], got.at[side, (r + NT - 1) % NT], k + side, to).start()

    def wide_wait(got, k):
        for side, _ in sides:
            remote(got.at[side], got.at[side], k + side, upper).wait_recv()

    def wide_sent(got, k):
        for side, _ in sides:
            remote(got.at[side], got.at[side], k + side, upper).wait_send()

    msg_h[0] = jnp.zeros_like(msg_h[0])
    msg_h[0, 0, 0:1, :] = msg_a0[16:17, :]
    msg_h[0, 0, 1:2, :] = msg_a0[ROWS + 16 : ROWS + 17, :]
    msg_h[0, 1, 0:1, :] = msg_a0[1:2, :]
    msg_h[0, 1, 1:2, :] = msg_a0[ROWS + 1 : ROWS + 2, :]
    wide_send(msg_h.at[0], got_h.at[0], 16)
    group_send(msg_a0, got_a0, 4)
    halo = [
        remote(spk_hbm.at[pl.ds(NEU - FR, FR), :], halo_spk.at[0], 0, upper),
        remote(spk_hbm.at[pl.ds(0, FR), :], halo_spk.at[1], 1, lower),
        remote(decay.at[pl.ds(8, 8), :], halo_dec.at[0], 2, upper),
        remote(decay.at[pl.ds(0, 8), :], halo_dec.at[1], 3, lower),
    ]
    for copy in halo:
        copy.start()

    lax.fori_loop(16, 32, arrange, 0, unroll=4)

    load_rec.wait()

    def turn(q, _):
        rec_t[q] = rec_raw[pl.ds(pl.multiple_of(q * PIX_BLOCK, PIX_BLOCK), PIX_BLOCK), :].T
        return 0

    lax.fori_loop(0, 32, turn, 0, unroll=8)

    for copy in halo:
        copy.wait_recv()
    decd[0:1, :] = halo_dec[0, 7:8, :]
    decd[17:18, :] = halo_dec[1, 0:1, :]
    has_lower = jnp.where(tile > 0, 1.0, 0.0)
    has_upper = jnp.where(tile < NTILE - 1, 1.0, 0.0)
    prepare(0, decd[0:1, :], has_lower, halo_spk[0], False)
    prepare(17, decd[17:18, :], has_upper, halo_spk[1], False)

    def cumulate(tri, out, first=0, last=NCOL // 2):
        def body(c, _):
            at = lanes(c, 256)
            out[:, at] = jnp.dot(tri[...], xh[:, at], preferred_element_type=F32)
            return 0

        lax.fori_loop(first, last, body, 0, unroll=last - first)

    def put_columns(value):
        def body(c, before):
            y = value(c)
            val_n[:, lanes(c)] = y.astype(BF16)
            turned = pltpu.roll(y, NEU_BLOCK, 1)
            val_s[:, lanes(c)] = jnp.where(low_half, before, turned).astype(BF16)
            return turned

        last = lax.fori_loop(0, NCOL, body, jnp.zeros((FR, FR), F32), unroll=6)
        val_s[:, NCOL * FR : (NCOL + 1) * FR] = last.astype(BF16)

    low_row = lax.broadcasted_iota(jnp.int32, (1, FR), 1) < NEU_BLOCK
    m_lo = jnp.where(low_row, 1.0, 0.0).astype(BF16)
    m_hi = jnp.where(low_row, 0.0, 1.0).astype(BF16)

    def pick(i):
        n0, n1, n2 = (val_n[:, lanes(i + k)] for k in range(3))
        s0, s1, s2 = (val_s[:, lanes(i + 1 + k)] for k in range(3))
        one_e, one_o = is_one(2 * i), is_one(2 * i + 1)

        def pair(x0, x1, x2, y, one):
            a = x0 * m_lo + y * m_hi
            first = jnp.where(low_row, 0.0, one).astype(BF16)
            second = jnp.where(low_row, 0.0, 1.0 - one).astype(BF16)
            b = x2 * m_lo + x0 * first + x1 * second
            return jnp.concatenate([a, b], axis=1)

        return pair(n0, n1, n2, s0, one_e), pair(s0, s1, s2, n1, one_o), one_e, one_o

    def model(i):
        even, odd, one_e, one_o = pick(i)
        y_e = jnp.dot(even, fpt[2 * i], preferred_element_type=F32)
        y_o = jnp.dot(odd, fpt[2 * i + 1], preferred_element_type=F32)
        return y_e, y_o, one_e, one_o

    def residual_step(i):
        y_e, y_o, one_e, one_o = model(i)
        r_e = (y_e - rec_t[2 * i].astype(F32)).astype(BF16)
        r_o = (y_o - rec_t[2 * i + 1].astype(F32)).astype(BF16)
        c = jnp.dot(r_e, fp[2 * i], preferred_element_type=F32)
        d = jnp.dot(r_o, fp[2 * i + 1], preferred_element_type=F32)
        ca, cb, da, db = c[:, :FR], c[:, FR:], d[:, :FR], d[:, FR:]
        acc_n[:, lanes(i)] += jnp.where(low_half, ca, cb * one_e)
        acc_s[:, lanes(i)] += jnp.where(low_half, da, ca + db * one_o)
        acc_n[:, lanes(i + 1)] += jnp.where(low_half, 0.0, cb * (1.0 - one_e) + da)
        acc_s[:, lanes(i + 1)] += jnp.where(low_half, 0.0, db * (1.0 - one_o))
        acc_n[:, lanes(i + 2)] += jnp.where(low_half, cb, 0.0)
        acc_s[:, lanes(i + 2)] += jnp.where(low_half, db, 0.0)

    def total_column(c, first=False):
        before = 0.0 if first else acc_s[:, lanes(c - 1)]
        return acc_n[:, lanes(c)] + pltpu.roll(jnp.where(low_half, acc_s[:, lanes(c)], before), NEU_BLOCK, 1)

    step = None
    for it in range(ITERS):
        msg_a, got_a, sem_a = (msg_a0, got_a0, 4) if it == 0 else (msg_a1, got_a1, 5)
        if it > 0:

            def update(c, _):
                at = lanes(c, 256)
                new = jnp.maximum(cur[:, at] - step * grad[:, at], 0.0)
                cur[:, at] = new
                x = inv[:, at] * new
                sums = jnp.sum(x, axis=0, keepdims=True)
                msg_a1[pl.ds(2 * c, 1), :] = sums[:, :FR]
                msg_a1[pl.ds(2 * c + 1, 1), :] = sums[:, FR:]
                hi, lo = split_rows(x)
                xh[0:FR, at] = hi
                xh[FR : 2 * FR, at] = lo
                return 0

            lax.fori_loop(0, NCOL // 2, update, 0, unroll=3)
            group_send(msg_a, got_a, sem_a)
        cumulate(tri_lo, loc)
        acc_n[...] = jnp.zeros_like(acc_n)
        acc_s[...] = jnp.zeros_like(acc_s)
        group_wait(got_a, sem_a)
        if it == 0:
            wide_wait(got_h.at[0], 16)
            for k in range(NT):
                for part, at in ((0, 0), (1, ROWS)):
                    got_a0[k, at : at + 1, :] = has_lower * got_h[0, 0, k, part : part + 1, :]
                    got_a0[k, at + 17 : at + 18, :] = has_upper * got_h[0, 1, k, part : part + 1, :]
            ld = jnp.log1p(decd[...] - 1.0)
            run = None
            for j in range(NT):
                tab = got_a0.at[slot_of(j)]
                tot = tab[ROWS + NCOL : ROWS + NCOL + 1, :]
                mid = tab[ROWS + NCOL + 1 : ROWS + NCOL + 2, :]
                tab_u[j] = jnp.exp(64.0 * ld + (tot - mid))
                tab_e[j] = jnp.exp(64.0 * ld + mid)
                tab_t[j] = jnp.exp(128.0 * ld + tot)
                tab_q[j] = tab_u[j] * tab[ROWS : 2 * ROWS, :]
            run = tab_e[tm]
            for j in range(NT - 1, -1, -1):
                active = j < tm
                tab_c[j] = jnp.where(active, run * tab_u[j], 0.0)
                run = jnp.where(active, run * tab_t[j], run)
        carry = jnp.zeros((ROWS, FR), F32)
        for j in range(NT):
            carry = carry + tab_c[j] * got_a[slot_of(j), 0:ROWS, :]
        row_c[...] = carry

        def traces_of(c):
            y = fwd[:, lanes(c)] * (loc[:, lanes(c)] + row_c[pl.ds(c, 1), :])
            if it == ITERS - 1:
                loc[:, lanes(c)] = y
            return y

        put_columns(traces_of)

        def edge_blocks(k, _):
            residual_step(k + 12 * lax.div(k, 2))
            return 0

        lax.fori_loop(0, 4, edge_blocks, 0, unroll=4)
        msg_b[2 * it, :, :FR] = total_column(0, first=True)
        msg_b[2 * it, :, FR:] = total_column(1)
        msg_b[2 * it + 1, :, :FR] = total_column(16)
        msg_b[2 * it + 1, :, FR:] = total_column(17)
        to_low = remote(msg_b.at[2 * it], got_b.at[2 * it], 6 + 2 * it, lower)
        to_up = remote(msg_b.at[2 * it + 1], got_b.at[2 * it + 1], 7 + 2 * it, upper)
        to_low.start()
        to_up.start()

        def sum_column(c, x):
            msg_cd[it, pl.ds(c, 1), :] = jnp.sum(x, axis=0, keepdims=True)
            msg_cd[it, pl.ds(ROWS + c, 1), :] = jnp.sum(x * sq[:, lanes(c)], axis=0, keepdims=True)

        def split_column(c, x):
            hi, lo = split_rows(x)
            xh[0:FR, lanes(c)] = hi
            xh[FR : 2 * FR, lanes(c)] = lo

        for c, part, half in ((0, 2 * it, 0), (1, 2 * it, 1), (16, 2 * it + 1, 0), (17, 2 * it + 1, 1)):
            sum_column(c, fwd[:, lanes(c)] * msg_b[part, :, half * FR : (half + 1) * FR])
        msg_h[1 + it] = jnp.zeros_like(msg_h[1 + it])
        for side, c in ((0, 16), (1, 0)):
            msg_h[1 + it, side, 0:2, :] = msg_cd[it, c : c + 2, :]
            msg_h[1 + it, side, 2:4, :] = msg_cd[it, ROWS + c : ROWS + c + 2, :]
        wide_send(msg_h.at[1 + it], got_h.at[1 + it], 18 + 2 * it)

        def inner_blocks(k, _):
            residual_step(k + 2)
            return 0

        lax.fori_loop(0, 12, inner_blocks, 0, unroll=12)

        def inner_column(k, _):
            x = fwd[:, lanes(k + 2)] * total_column(k + 2)
            sum_column(k + 2, x)
            split_column(k + 2, x)
            return 0

        lax.fori_loop(0, 14, inner_column, 0, unroll=7)
        group_send(msg_cd.at[it], got_cd.at[it], 10 + it)
        cumulate(tri_up, loc2, 1, 8)
        to_low.wait_recv()
        to_up.wait_recv()
        for c, part, present in ((0, 2 * it + 1, has_lower), (16, 2 * it, has_upper)):
            for half in range(2):
                at = slice(half * FR, (half + 1) * FR)
                mine = msg_b[2 * it if c == 0 else 2 * it + 1, :, at]
                split_column(c + half, fwd[:, lanes(c + half)] * (mine + present * got_b[part, :, at]))
        cumulate(tri_up, loc2, 0, 1)
        cumulate(tri_up, loc2, 8, 9)

        def square_part(c, _):
            at = lanes(c, 256)
            a = inv[:, at]
            hi, lo = split_rows(a * a * loc2[:, at])
            both = jnp.concatenate([hi, lo], axis=0)
            grad[:, at] = jnp.dot(tri_lo[...], both, preferred_element_type=F32)
            return 0

        lax.fori_loop(0, NCOL // 2, square_part, 0, unroll=9)
        group_wait(got_cd.at[it], 10 + it)
        wide_wait(got_h.at[1 + it], 18 + 2 * it)
        for k in range(NT):
            for part, at in ((0, 0), (2, ROWS)):
                got_cd[it, k, at : at + 2, :] += has_lower * got_h[1 + it, 0, k, part : part + 2, :]
                got_cd[it, k, at + 16 : at + 18, :] += has_upper * got_h[1 + it, 1, k, part : part + 2, :]
        w = jnp.zeros((ROWS, FR), F32)
        mine = w
        carry = w
        for j in range(NT - 1, -1, -1):
            at = slot_of(j)
            mine = jnp.where(tm == j, w, mine)
            carry = carry + tab_c[j] * (got_cd[it, at, ROWS : 2 * ROWS, :] + tab_q[j] * w)
            w = tab_e[j] * got_cd[it, at, 0:ROWS, :] + tab_t[j] * w
        row_w[...] = tab_u[tm] * mine
        row_c[...] = carry

        def direction_of(c):
            at = lanes(c)
            return fwd[:, at] * (grad[:, at] + sq[:, at] * row_w[pl.ds(c, 1), :] + row_c[pl.ds(c, 1), :])

        put_columns(direction_of)

        def gradient_column(c):
            at = lanes(c)
            g = inv[:, at] * (loc2[:, at] + row_w[pl.ds(c, 1), :])
            grad[:, at] = g
            return g

        def image_step(i, sums):
            g_sum, p_sum = sums
            y_e, y_o, _, _ = model(i)
            p = y_e * y_e + y_o * y_o
            p_sum = p_sum + jnp.sum(p.reshape(16, 8, 256), axis=0)
            g = gradient_column(i + 1)
            g_sum = g_sum + jnp.sum((g * g).reshape(16, 8, FR), axis=0)
            return g_sum, p_sum

        g_sum, p_sum = lax.fori_loop(
            0, 16, image_step, (jnp.zeros((8, FR), F32), jnp.zeros((8, 2 * FR), F32)), unroll=16
        )
        g_row = jnp.sum(g_sum, axis=0, keepdims=True)
        p_row = jnp.sum(p_sum[:, :FR] + p_sum[:, FR:], axis=0, keepdims=True)
        total = jnp.where(
            low_row, g_row + pltpu.roll(g_row, NEU_BLOCK, 1), p_row + pltpu.roll(p_row, NEU_BLOCK, 1)
        )
        for k, (stage, got_e) in enumerate(zip(STAGES, (got_e0, got_e1))):
            msg_e[2 * it + k] = total
            n = len(stage)
            for i, o in enumerate(stage):
                remote(msg_e.at[2 * it + k], got_e.at[it, i], 12 + 2 * it + k, device_at(o)).start()
            if k == 0:
                if it < ITERS - 1:
                    gradient_column(0)
                    gradient_column(17)
            elif it == ITERS - 1:

                def turn_out(c, _):
                    at = lanes(c + 1)
                    to = pl.ds(pl.multiple_of(c * FR, FR), FR)
                    out_tr[to, :] = loc[:, at].T
                    spk_raw[to, :] = cur[:, at].T
                    rec32 = grad[:, at].T
                    out_spk[to, :] = rec32
                    return 0

                lax.fori_loop(0, 16, turn_out, 0, unroll=4)
            everything = got_e.at[it]
            remote(everything, everything, 12 + 2 * it + k, upper).wait_recv()
            parts = [total] + [got_e[it, i] for i in range(n)]
            while len(parts) > 1:
                parts = [a + b for a, b in zip(parts[::2], parts[1::2])] + parts[len(parts) // 2 * 2 :]
            total = parts[0]
        grad_sq = jnp.sum(jnp.where(low_row, total, 0.0), axis=1, keepdims=True)
        image_sq = jnp.sum(jnp.where(low_row, 0.0, total), axis=1, keepdims=True)
        step = grad_sq / (image_sq + 1e-06)

    def finish(c, _):
        to = pl.ds(pl.multiple_of(c * 256, 256), 256)
        out_spk[to, :] = jnp.maximum(spk_raw[to, :] - step * out_spk[to, :], 0.0)
        return 0

    lax.fori_loop(0, 8, finish, 0, unroll=4)

    for copy in halo:
        copy.wait_send()
    group_sent(got_a0, 4)
    group_sent(got_a1, 5)
    for k in range(1 + ITERS):
        wide_sent(got_h.at[k], 16 + 2 * k)
    for it in range(ITERS):
        remote(msg_b.at[2 * it], got_b.at[2 * it], 6 + 2 * it, lower).wait_send()
        remote(msg_b.at[2 * it + 1], got_b.at[2 * it + 1], 7 + 2 * it, upper).wait_send()
        group_sent(got_cd.at[it], 10 + it)
        for k, got_e in enumerate((got_e0, got_e1)):
            everything = got_e.at[it]
            remote(everything, everything, 12 + 2 * it + k, upper).wait_send()


def per_device(recording, footprints, pattern, decay, frame_gain, spikes):
    wide = (FR, NCOL * FR)
    vm = pltpu.VMEM
    scratch = [
        vm((PIX, 256), BF16), vm((PIX, FR), BF16), vm((NEU, FR), F32),
        vm((16, FR), F32), vm((1, FR), F32), pltpu.SMEM((K, 32), jnp.int32),
        vm((32, 256, 256), BF16), vm((32, 256, 256), BF16), vm((32, FR, 256), BF16),
        vm(wide, F32), vm(wide, F32), vm(wide, F32), vm(wide, F32), vm(wide, F32),
        vm((2 * FR, NCOL * FR), BF16), vm(wide, F32), vm(wide, F32), vm(wide, F32), vm(wide, F32),
        vm(wide, BF16), vm((FR, (NCOL + 1) * FR), BF16),
        vm((FR, FR), F32), vm((FR, 2 * FR), BF16), vm((FR, 2 * FR), BF16),
        vm((ROWS, FR), F32),
        vm((NT, ROWS, FR), F32), vm((NT, ROWS, FR), F32), vm((NT, ROWS, FR), F32),
        vm((NT, ROWS, FR), F32), vm((NT, ROWS, FR), F32),
        vm((ROWS, FR), F32), vm((ROWS, FR), F32),
        vm((2, FR, FR), F32), vm((2, 8, FR), F32),
        vm((2 * ROWS, FR), F32), vm((ROWS, FR), F32), vm((ITERS, 2 * ROWS, FR), F32),
        vm((NT, 2 * ROWS, FR), F32), vm((NT, ROWS, FR), F32), vm((ITERS, NT, 2 * ROWS, FR), F32),
        vm((2 * ITERS, FR, 2 * FR), F32), vm((2 * ITERS, FR, 2 * FR), F32),
        vm((1 + ITERS, 2, 8, FR), F32), vm((1 + ITERS, 2, NT, 8, FR), F32),
        vm((2 * ITERS, 1, FR), F32),
        vm((ITERS, len(STAGES[0]), 1, FR), F32), vm((ITERS, len(STAGES[1]), 1, FR), F32),
        pltpu.SemaphoreType.DMA((22,)), pltpu.SemaphoreType.DMA((22,)), pltpu.SemaphoreType.DMA((6,)),
    ]
    anywhere = pl.BlockSpec(memory_space=pl.ANY)
    in_vmem = pl.BlockSpec(memory_space=pltpu.VMEM)
    return pl.pallas_call(
        kernel,
        out_shape=(pltpu.VMEM((NEU, FR), F32), pltpu.VMEM((NEU, FR), F32)),
        in_specs=[
            anywhere, anywhere, anywhere, anywhere, anywhere, anywhere,
        ],
        out_specs=(in_vmem, in_vmem),
        scratch_shapes=scratch,
        compiler_params=pltpu.CompilerParams(
            collective_id=0, has_side_effects=True, vmem_limit_bytes=60 * 2**20
        ),
        name="deconvolve",
    )(
        recording, footprints, pattern.T, decay.reshape(16, FR), frame_gain.reshape(1, FR), spikes,
    )


def solution(mesh):
    return jax.shard_map(
        per_device,
        mesh=mesh,
        in_specs=(
            P("tile", "tm"),
            P("tile", None),
            P("tile", None),
            P("tile"),
            P("tm"),
            P("tile", "tm"),
        ),
        out_specs=(P("tile", "tm"), P("tile", "tm")),
        check_vma=False,
    )
```

```python
import functools
import itertools

import jax
import jax.numpy as jnp
from jax import lax
from jax.experimental import pallas as pl
from jax.experimental.pallas import tpu as pltpu
from jax.sharding import PartitionSpec as P

NEU_BLOCK = 64
PIX_BLOCK = 256
K = 4
HB = 2
ITERS = 2

NX, NY, NZ, NC = 4, 4, 8, 2
NT = NX * NC
NTILE = NY * NZ
FR = 128
NCOL = 18
ROWS = 24
NEU = 2048
PIX = 8192
MESH = pl.DeviceIdType.MESH
F32 = jnp.float32
BF16 = jnp.bfloat16


def ring_distance(d, n):
    return min(d, n - d)


def offsets(keep):
    found = []
    for dx, dy, dz, dc in itertools.product(range(NX), range(NY), range(NZ), range(NC)):
        if (dx, dy, dz, dc) != (0, 0, 0, 0) and keep(dx, dy, dz, dc):
            far = ring_distance(dx, NX) + ring_distance(dy, NY) + ring_distance(dz, NZ)
            found.append((-far, dx, dy, dz, dc))
    return [o[1:] for o in sorted(found)]


TM_GROUP = offsets(lambda dx, dy, dz, dc: dy == 0 and dz == 0)
CORE_GROUP = offsets(lambda dx, dy, dz, dc: dx == 0 and dy == 0 and dz == 0)
CHIP_GROUP = offsets(lambda dx, dy, dz, dc: dc == 0)
STAGES = (CORE_GROUP, CHIP_GROUP)


def split_rows(x):
    hi = x.astype(BF16)
    lo = (x - hi.astype(F32)).astype(BF16)
    return hi, lo


def kernel(
    rec_hbm, foot_hbm, pat_hbm, dec_hbm, gain_hbm, spk_hbm,
    out_spk, out_tr,
    foot_raw, rec_raw, spk_raw, decay, fgain, pat, fp, fpt, rec_t,
    cur, grad, fwd, inv, sq, xh, loc, loc2, acc_n, acc_s, val_n, val_s,
    seam, lgb, tri_lo, tri_up, decd, tab_u, tab_e, tab_t, tab_q, tab_c, row_w, row_c,
    halo_spk, halo_dec, msg_a0, msg_a1, msg_cda, msg_cdb, got_a0, got_a1, got_cda, got_cdb,
    msg_b, got_b, msg_h, got_h, msg_e, got_e0, got_e1,
    ss, rs, ls,
):
    tm = lax.axis_index("tm")
    tile = lax.axis_index("tile")
    px, pc = lax.div(tm, NC), lax.rem(tm, NC)
    py, pz = lax.div(tile, NZ), lax.rem(tile, NZ)

    def device_at(o):
        dx, dy, dz, dc = o
        x = lax.rem(px + dx, NX) if dx else px
        c = lax.rem(pc + dc, NC) if dc else pc
        y = lax.rem(py + dy, NY) if dy else py
        z = lax.rem(pz + dz, NZ) if dz else pz
        return (x * NC + c, y * NZ + z)

    upper = (tm, lax.rem(tile + 1, NTILE))
    lower = (tm, lax.rem(tile + NTILE - 1, NTILE))

    group = offsets(lambda *o: o in TM_GROUP or o in CORE_GROUP or o in CHIP_GROUP)
    sides = ((0, 1), (1, NTILE - 1))
    crossed = [(lax.rem(tm + k, NT), lax.rem(tile + by, NTILE)) for _, by in sides for k in range(1, NT, 2)]
    barrier = pltpu.get_barrier_semaphore()
    for o in group:
        pl.semaphore_signal(barrier, inc=1, device_id=device_at(o), device_id_type=MESH)
    for d in crossed:
        pl.semaphore_signal(barrier, inc=1, device_id=d, device_id_type=MESH)

    load_dec = pltpu.make_async_copy(dec_hbm, decay, ls.at[3])
    load_gain = pltpu.make_async_copy(gain_hbm, fgain, ls.at[4])
    load_pat = pltpu.make_async_copy(pat_hbm, pat, ls.at[5])
    load_spk = pltpu.make_async_copy(spk_hbm, spk_raw, ls.at[0])
    load_foot = pltpu.make_async_copy(foot_hbm, foot_raw, ls.at[1])
    load_rec = pltpu.make_async_copy(rec_hbm, rec_raw, ls.at[2])
    for load in (load_dec, load_gain, load_pat, load_spk, load_foot, load_rec):
        load.start()

    def lanes(c, width=128):
        return pl.ds(pl.multiple_of(c * width, width), width)

    row = lax.broadcasted_iota(jnp.int32, (FR, FR), 0)
    col = lax.broadcasted_iota(jnp.int32, (FR, FR), 1)
    low_half = col < NEU_BLOCK
    t_centred = (row - 63).astype(F32)

    lower_tri = (row >= col).astype(BF16)
    upper_tri = (row <= col).astype(BF16)
    tri_lo[:, :FR] = lower_tri
    tri_lo[:, FR:] = lower_tri
    tri_up[:, :FR] = upper_tri
    tri_up[:, FR:] = upper_tri

    load_gain.wait()
    log_fg = jnp.log(fgain[...])
    lg = jnp.sum(jnp.where(row >= col, log_fg, 0.0), axis=1, keepdims=True)
    lg_mid = lg[63:64, :]
    lg_tot = lg[127:128, :]
    lgb[...] = jnp.broadcast_to(lg - lg_mid, (FR, FR))

    msg_a0[...] = jnp.zeros_like(msg_a0)
    msg_a1[...] = jnp.zeros_like(msg_a1)
    msg_cda[...] = jnp.zeros_like(msg_cda)
    msg_cdb[...] = jnp.zeros_like(msg_cdb)
    msg_a0[ROWS + NCOL : ROWS + NCOL + 1, :] = jnp.broadcast_to(lg_tot, (1, FR))
    msg_a0[ROWS + NCOL + 1 : ROWS + NCOL + 2, :] = jnp.broadcast_to(lg_mid, (1, FR))
    decd[...] = jnp.ones_like(decd)
    load_dec.wait()
    decd[1:17, :] = decay[...]

    def prepare(c, d, present, block, own):
        ld = jnp.log1p(d - 1.0)
        gain = jnp.sqrt(1.0 - d * d) * present
        lc = t_centred * ld + lgb[...]
        f = jnp.exp(lc)
        a = gain * jnp.exp(-lc)
        fwd[:, lanes(c)] = f
        inv[:, lanes(c)] = a
        hi, lo = split_rows(a * a)
        s2 = jnp.dot(tri_lo[...], jnp.concatenate([hi, lo], axis=0), preferred_element_type=F32)
        sq[:, lanes(c)] = s2
        if own:
            msg_a0[pl.ds(ROWS + c, 1), :] = s2[FR - 1 : FR, :]
        s = block.T
        cur[:, lanes(c)] = s
        x = a * s
        if own:
            msg_a0[pl.ds(c, 1), :] = jnp.sum(x, axis=0, keepdims=True)
        hi, lo = split_rows(x)
        xh[0:FR, lanes(c)] = hi
        xh[FR : 2 * FR, lanes(c)] = lo

    load_spk.wait()

    def own_column(k, _):
        prepare(k + 1, decd[pl.ds(k + 1, 1), :], 1.0, spk_raw[pl.ds(pl.multiple_of(k * FR, FR), FR), :], True)
        return 0

    lax.fori_loop(0, 16, own_column, 0, unroll=4)

    def names(q, k, v):
        return jnp.where(pat[k, q] - q == v, 1.0, 0.0)

    def sources(q):
        own = [[names(q, k, v) for k in range(K)] for v in (0, 2, 4)]
        return own + [[1.0 - own[0][k] - own[1][k] - own[2][k] for k in range(K)]]

    def is_one(q):
        return sum(names(q, k, 1) for k in range(K))

    load_pat.wait()
    load_foot.wait()

    def arrange(q, _):
        at = pl.ds(pl.multiple_of(q * PIX_BLOCK, PIX_BLOCK), PIX_BLOCK)
        turned = foot_raw[at, :].T
        chunks = [turned[k * NEU_BLOCK : (k + 1) * NEU_BLOCK, :] for k in range(K)]
        for s, weights in enumerate(sources(q)):
            mixed = sum(chunks[k] * jnp.full((1, PIX_BLOCK), weights[k], F32).astype(BF16) for k in range(K))
            fpt[q, s * NEU_BLOCK : (s + 1) * NEU_BLOCK, :] = mixed
        fp[q] = fpt[q].T
        return 0


    lax.fori_loop(0, 16, arrange, 0, unroll=4)

    pl.semaphore_wait(barrier, len(group) + len(crossed))

    def remote(src, dst, k, device):
        return pltpu.make_async_remote_copy(
            src_ref=src, dst_ref=dst, send_sem=ss.at[k], recv_sem=rs.at[k],
            device_id=device, device_id_type=MESH,
        )

    def group_send(src, got, k):
        for r in range(1, NT):
            remote(src, got.at[r - 1], k, (lax.rem(tm + r, NT), tile)).start()
        got[NT - 1] = src[...]

    def group_wait(got, k):
        part = got.at[pl.ds(0, NT - 1)]
        remote(part, part, k, upper).wait_recv()

    def group_sent(got, k):
        part = got.at[pl.ds(0, NT - 1)]
        remote(part, part, k, upper).wait_send()

    def slot_of(j):
        return lax.rem(tm - j + NT - 1, NT)

    def wide_send(src, got, k):
        for side, by in sides:
            for r in range(NT):
                to = (lax.rem(tm + r, NT), lax.rem(tile + by, NTILE))
                remote(src.at[side], got.at[side, (r + NT - 1) % NT], k + side, to).start()

    def wide_wait(got, k):
        for side, _ in sides:
            remote(got.at[side], got.at[side], k + side, upper).wait_recv()

    def wide_sent(got, k):
        for side, _ in sides:
            remote(got.at[side], got.at[side], k + side, upper).wait_send()

    msg_h[0] = jnp.zeros_like(msg_h[0])
    msg_h[0, 0, 0:1, :] = msg_a0[16:17, :]
    msg_h[0, 0, 1:2, :] = msg_a0[ROWS + 16 : ROWS + 17, :]
    msg_h[0, 1, 0:1, :] = msg_a0[1:2, :]
    msg_h[0, 1, 1:2, :] = msg_a0[ROWS + 1 : ROWS + 2, :]
    wide_send(msg_h.at[0], got_h.at[0], 16)
    group_send(msg_a0, got_a0, 4)
    halo = [
        remote(spk_hbm.at[pl.ds(NEU - FR, FR), :], halo_spk.at[0], 0, upper),
        remote(spk_hbm.at[pl.ds(0, FR), :], halo_spk.at[1], 1, lower),
        remote(decay.at[pl.ds(8, 8), :], halo_dec.at[0], 2, upper),
        remote(decay.at[pl.ds(0, 8), :], halo_dec.at[1], 3, lower),
    ]
    for copy in halo:
        copy.start()

    lax.fori_loop(16, 32, arrange, 0, unroll=4)

    load_rec.wait()

    def turn(q, _):
        rec_t[q] = rec_raw[pl.ds(pl.multiple_of(q * PIX_BLOCK, PIX_BLOCK), PIX_BLOCK), :].T
        return 0

    lax.fori_loop(0, 32, turn, 0, unroll=8)

    for copy in halo:
        copy.wait_recv()
    decd[0:1, :] = halo_dec[0, 7:8, :]
    decd[17:18, :] = halo_dec[1, 0:1, :]
    has_lower = jnp.where(tile > 0, 1.0, 0.0)
    has_upper = jnp.where(tile < NTILE - 1, 1.0, 0.0)
    prepare(0, decd[0:1, :], has_lower, halo_spk[0], False)
    prepare(17, decd[17:18, :], has_upper, halo_spk[1], False)

    def cumulate(tri, out, first=0, last=NCOL // 2):
        def body(c, _):
            at = lanes(c, 256)
            out[:, at] = jnp.dot(tri[...], xh[:, at], preferred_element_type=F32)
            return 0

        lax.fori_loop(first, last, body, 0, unroll=last - first)

    def put_column(c, y, before):
        val_n[:, lanes(c)] = y.astype(BF16)
        turned = pltpu.roll(y, NEU_BLOCK, 1)
        val_s[:, lanes(c)] = jnp.where(low_half, before, turned).astype(BF16)
        return turned

    def put_moved(c, turned, after):
        val_s[:, lanes(c + 1)] = jnp.where(low_half, turned, after).astype(BF16)

    nothing = jnp.zeros((FR, FR), F32)

    low_row = lax.broadcasted_iota(jnp.int32, (1, FR), 1) < NEU_BLOCK
    m_lo = jnp.where(low_row, 1.0, 0.0).astype(BF16)
    m_hi = jnp.where(low_row, 0.0, 1.0).astype(BF16)

    def pick(i):
        n0, n1, n2 = (val_n[:, lanes(i + k)] for k in range(3))
        s0, s1, s2 = (val_s[:, lanes(i + 1 + k)] for k in range(3))
        one_e, one_o = is_one(2 * i), is_one(2 * i + 1)

        def pair(x0, x1, x2, y, one):
            a = x0 * m_lo + y * m_hi
            first = jnp.where(low_row, 0.0, one).astype(BF16)
            second = jnp.where(low_row, 0.0, 1.0 - one).astype(BF16)
            b = x2 * m_lo + x0 * first + x1 * second
            return jnp.concatenate([a, b], axis=1)

        return pair(n0, n1, n2, s0, one_e), pair(s0, s1, s2, n1, one_o), one_e, one_o

    def model(i):
        even, odd, one_e, one_o = pick(i)
        y_e = jnp.dot(even, fpt[2 * i], preferred_element_type=F32)
        y_o = jnp.dot(odd, fpt[2 * i + 1], preferred_element_type=F32)
        return y_e, y_o, one_e, one_o

    def residual_step(i):
        y_e, y_o, one_e, one_o = model(i)
        r_e = (y_e - rec_t[2 * i].astype(F32)).astype(BF16)
        r_o = (y_o - rec_t[2 * i + 1].astype(F32)).astype(BF16)
        c = jnp.dot(r_e, fp[2 * i], preferred_element_type=F32)
        d = jnp.dot(r_o, fp[2 * i + 1], preferred_element_type=F32)
        ca, cb, da, db = c[:, :FR], c[:, FR:], d[:, :FR], d[:, FR:]
        acc_n[:, lanes(i)] += jnp.where(low_half, ca, cb * one_e)
        acc_s[:, lanes(i)] += jnp.where(low_half, da, ca + db * one_o)
        acc_n[:, lanes(i + 1)] += jnp.where(low_half, 0.0, cb * (1.0 - one_e) + da)
        acc_s[:, lanes(i + 1)] += jnp.where(low_half, 0.0, db * (1.0 - one_o))
        acc_n[:, lanes(i + 2)] += jnp.where(low_half, cb, 0.0)
        acc_s[:, lanes(i + 2)] += jnp.where(low_half, db, 0.0)

    def total_column(c, first=False):
        before = 0.0 if first else acc_s[:, lanes(c - 1)]
        return acc_n[:, lanes(c)] + pltpu.roll(jnp.where(low_half, acc_s[:, lanes(c)], before), NEU_BLOCK, 1)

    step = None
    for it in range(ITERS):
        msg_a, got_a, sem_a = (msg_a0, got_a0, 4) if it == 0 else (msg_a1, got_a1, 5)
        if it > 0:

            def update(c, _):
                at = lanes(c, 256)
                new = jnp.maximum(cur[:, at] - step * grad[:, at], 0.0)
                cur[:, at] = new
                x = inv[:, at] * new
                sums = jnp.sum(x, axis=0, keepdims=True)
                msg_a1[pl.ds(2 * c, 1), :] = sums[:, :FR]
                msg_a1[pl.ds(2 * c + 1, 1), :] = sums[:, FR:]
                hi, lo = split_rows(x)
                xh[0:FR, at] = hi
                xh[FR : 2 * FR, at] = lo
                return 0

            lax.fori_loop(0, NCOL // 2, update, 0, unroll=3)
            group_send(msg_a, got_a, sem_a)
        cumulate(tri_lo, loc)
        acc_n[...] = jnp.zeros_like(acc_n)
        acc_s[...] = jnp.zeros_like(acc_s)
        group_wait(got_a, sem_a)
        if it == 0:
            wide_wait(got_h.at[0], 16)
            for k in range(NT):
                for part, at in ((0, 0), (1, ROWS)):
                    got_a0[k, at : at + 1, :] = has_lower * got_h[0, 0, k, part : part + 1, :]
                    got_a0[k, at + 17 : at + 18, :] = has_upper * got_h[0, 1, k, part : part + 1, :]
            ld = jnp.log1p(decd[...] - 1.0)
            run = None
            for j in range(NT):
                tab = got_a0.at[slot_of(j)]
                tot = tab[ROWS + NCOL : ROWS + NCOL + 1, :]
                mid = tab[ROWS + NCOL + 1 : ROWS + NCOL + 2, :]
                tab_u[j] = jnp.exp(64.0 * ld + (tot - mid))
                tab_e[j] = jnp.exp(64.0 * ld + mid)
                tab_t[j] = jnp.exp(128.0 * ld + tot)
                tab_q[j] = tab_u[j] * tab[ROWS : 2 * ROWS, :]
            run = tab_e[tm]
            for j in range(NT - 1, -1, -1):
                active = j < tm
                tab_c[j] = jnp.where(active, run * tab_u[j], 0.0)
                run = jnp.where(active, run * tab_t[j], run)
        carry = jnp.zeros((ROWS, FR), F32)
        for j in range(NT):
            carry = carry + tab_c[j] * got_a[slot_of(j), 0:ROWS, :]
        row_c[...] = carry

        def traces_of(c):
            y = fwd[:, lanes(c)] * (loc[:, lanes(c)] + row_c[pl.ds(c, 1), :])
            if it == ITERS - 1:
                loc[:, lanes(c)] = y
            return y

        def put_trace(c, before):
            return put_column(c, traces_of(c), before)

        def put_and_step(c, before):
            turned = put_trace(c, before)
            residual_step(c - 3)
            return turned

        def step_only(i, _):
            residual_step(i)
            return 0

        seam[0] = lax.fori_loop(0, 5, put_trace, nothing, unroll=5)
        lax.fori_loop(0, 2, step_only, 0, unroll=2)
        seam[1] = put_trace(14, nothing)
        put_moved(17, lax.fori_loop(15, NCOL, put_trace, seam[1], unroll=3), nothing)
        lax.fori_loop(14, 16, step_only, 0, unroll=2)
        msg_b[2 * it, :, :FR] = total_column(0, first=True)
        msg_b[2 * it, :, FR:] = total_column(1)
        msg_b[2 * it + 1, :, :FR] = total_column(16)
        msg_b[2 * it + 1, :, FR:] = total_column(17)
        to_low = remote(msg_b.at[2 * it], got_b.at[2 * it], 6 + 2 * it, lower)
        to_up = remote(msg_b.at[2 * it + 1], got_b.at[2 * it + 1], 7 + 2 * it, upper)
        to_low.start()
        to_up.start()

        parts_cd = ((msg_cda, got_cda, 0, 8, 10 + it), (msg_cdb, got_cdb, 8, 16, 22 + it))

        def sum_column(c, x, part):
            msg, _, base, n, _ = parts_cd[part]
            msg[it, pl.ds(c - base, 1), :] = jnp.sum(x, axis=0, keepdims=True)
            msg[it, pl.ds(n + c - base, 1), :] = jnp.sum(x * sq[:, lanes(c)], axis=0, keepdims=True)

        def split_column(c, x):
            hi, lo = split_rows(x)
            xh[0:FR, lanes(c)] = hi
            xh[FR : 2 * FR, lanes(c)] = lo

        for c, part, half in ((0, 2 * it, 0), (1, 2 * it, 1), (16, 2 * it + 1, 0), (17, 2 * it + 1, 1)):
            sum_column(c, fwd[:, lanes(c)] * msg_b[part, :, half * FR : (half + 1) * FR], part - 2 * it)
        msg_h[1 + it] = jnp.zeros_like(msg_h[1 + it])
        msg_h[1 + it, 0, 0:2, :] = msg_cdb[it, 8:10, :]
        msg_h[1 + it, 0, 2:4, :] = msg_cdb[it, 24:26, :]
        msg_h[1 + it, 1, 0:2, :] = msg_cda[it, 0:2, :]
        msg_h[1 + it, 1, 2:4, :] = msg_cda[it, 8:10, :]
        wide_send(msg_h.at[1 + it], got_h.at[1 + it], 18 + 2 * it)

        def inner_columns(first, last, part):
            def inner_column(c, _):
                x = fwd[:, lanes(c)] * total_column(c)
                sum_column(c, x, part)
                split_column(c, x)
                return 0

            lax.fori_loop(first, last, inner_column, 0, unroll=last - first)
            msg, got, _, _, k = parts_cd[part]
            group_send(msg.at[it], got.at[it], k)

        before = lax.fori_loop(5, 11, put_and_step, seam[0], unroll=6)
        inner_columns(2, 8, 0)
        put_moved(13, lax.fori_loop(11, 14, put_and_step, before, unroll=3), seam[1])
        lax.fori_loop(11, 14, step_only, 0, unroll=3)
        inner_columns(8, 16, 1)
        cumulate(tri_up, loc2, 1, 8)
        to_low.wait_recv()
        to_up.wait_recv()
        for c, part, present in ((0, 2 * it + 1, has_lower), (16, 2 * it, has_upper)):
            for half in range(2):
                at = slice(half * FR, (half + 1) * FR)
                mine = msg_b[2 * it if c == 0 else 2 * it + 1, :, at]
                split_column(c + half, fwd[:, lanes(c + half)] * (mine + present * got_b[part, :, at]))
        cumulate(tri_up, loc2, 0, 1)
        cumulate(tri_up, loc2, 8, 9)

        def square_part(c, _):
            at = lanes(c, 256)
            a = inv[:, at]
            hi, lo = split_rows(a * a * loc2[:, at])
            both = jnp.concatenate([hi, lo], axis=0)
            grad[:, at] = jnp.dot(tri_lo[...], both, preferred_element_type=F32)
            return 0

        lax.fori_loop(0, NCOL // 2, square_part, 0, unroll=9)
        def carries(part):
            _, got, base, n, k = parts_cd[part]
            group_wait(got.at[it], k)
            at = part * 8
            present = (has_lower, has_upper)[part]
            for k in range(NT):
                got[it, k, at : at + 2, :] += present * got_h[1 + it, part, k, 0:2, :]
                got[it, k, n + at : n + at + 2, :] += present * got_h[1 + it, part, k, 2:4, :]
            rows = slice(base, base + n)
            w = jnp.zeros((n, FR), F32)
            mine = w
            carry = w
            for j in range(NT - 1, -1, -1):
                at = slot_of(j)
                mine = jnp.where(tm == j, w, mine)
                carry = carry + tab_c[j, rows, :] * (got[it, at, n : 2 * n, :] + tab_q[j, rows, :] * w)
                w = tab_e[j, rows, :] * got[it, at, 0:n, :] + tab_t[j, rows, :] * w
            row_w[rows, :] = tab_u[tm, rows, :] * mine
            row_c[rows, :] = carry

        wide_wait(got_h.at[1 + it], 18 + 2 * it)
        carries(0)

        def direction_of(c):
            at = lanes(c)
            return fwd[:, at] * (grad[:, at] + sq[:, at] * row_w[pl.ds(c, 1), :] + row_c[pl.ds(c, 1), :])

        def gradient_column(c):
            at = lanes(c)
            g = inv[:, at] * (loc2[:, at] + row_w[pl.ds(c, 1), :])
            grad[:, at] = g
            return g

        def image_step(i, sums):
            g_sum, p_sum = sums
            y_e, y_o, _, _ = model(i)
            p = y_e * y_e + y_o * y_o
            p_sum = p_sum + jnp.sum(p.reshape(16, 8, 256), axis=0)
            g = gradient_column(i + 1)
            g_sum = g_sum + jnp.sum((g * g).reshape(16, 8, FR), axis=0)
            return g_sum, p_sum

        def put_direction(c, before):
            return put_column(c, direction_of(c), before)

        def put_and_image(c, carried):
            before, g_sum, p_sum = carried
            turned = put_direction(c, before)
            return (turned,) + image_step(c - 3, (g_sum, p_sum))

        before = lax.fori_loop(0, 3, put_direction, nothing, unroll=3)
        carried = (before, jnp.zeros((8, FR), F32), jnp.zeros((8, 2 * FR), F32))
        carried = lax.fori_loop(3, 8, put_and_image, carried, unroll=5)
        carries(1)
        before, g_sum, p_sum = lax.fori_loop(8, NCOL, put_and_image, carried, unroll=10)
        put_moved(17, before, nothing)
        g_sum, p_sum = image_step(15, (g_sum, p_sum))
        g_row = jnp.sum(g_sum, axis=0, keepdims=True)
        p_row = jnp.sum(p_sum[:, :FR] + p_sum[:, FR:], axis=0, keepdims=True)
        total = jnp.where(
            low_row, g_row + pltpu.roll(g_row, NEU_BLOCK, 1), p_row + pltpu.roll(p_row, NEU_BLOCK, 1)
        )
        for k, (stage, got_e) in enumerate(zip(STAGES, (got_e0, got_e1))):
            msg_e[2 * it + k] = total
            n = len(stage)
            for i, o in enumerate(stage):
                remote(msg_e.at[2 * it + k], got_e.at[it, i], 12 + 2 * it + k, device_at(o)).start()
            if k == 0:
                if it < ITERS - 1:
                    gradient_column(0)
                    gradient_column(17)
            elif it == ITERS - 1:

                def turn_out(c, _):
                    at = lanes(c + 1)
                    to = pl.ds(pl.multiple_of(c * FR, FR), FR)
                    out_tr[to, :] = loc[:, at].T
                    spk_raw[to, :] = cur[:, at].T
                    rec32 = grad[:, at].T
                    out_spk[to, :] = rec32
                    return 0

                lax.fori_loop(0, 16, turn_out, 0, unroll=4)
            everything = got_e.at[it]
            remote(everything, everything, 12 + 2 * it + k, upper).wait_recv()
            parts = [total] + [got_e[it, i] for i in range(n)]
            while len(parts) > 1:
                parts = [a + b for a, b in zip(parts[::2], parts[1::2])] + parts[len(parts) // 2 * 2 :]
            total = parts[0]
        grad_sq = jnp.sum(jnp.where(low_row, total, 0.0), axis=1, keepdims=True)
        image_sq = jnp.sum(jnp.where(low_row, 0.0, total), axis=1, keepdims=True)
        step = grad_sq / (image_sq + 1e-06)

    def finish(c, _):
        to = pl.ds(pl.multiple_of(c * 256, 256), 256)
        out_spk[to, :] = jnp.maximum(spk_raw[to, :] - step * out_spk[to, :], 0.0)
        return 0

    lax.fori_loop(0, 8, finish, 0, unroll=4)

    for copy in halo:
        copy.wait_send()
    group_sent(got_a0, 4)
    group_sent(got_a1, 5)
    for k in range(1 + ITERS):
        wide_sent(got_h.at[k], 16 + 2 * k)
    for it in range(ITERS):
        remote(msg_b.at[2 * it], got_b.at[2 * it], 6 + 2 * it, lower).wait_send()
        remote(msg_b.at[2 * it + 1], got_b.at[2 * it + 1], 7 + 2 * it, upper).wait_send()
        group_sent(got_cda.at[it], 10 + it)
        group_sent(got_cdb.at[it], 22 + it)
        for k, got_e in enumerate((got_e0, got_e1)):
            everything = got_e.at[it]
            remote(everything, everything, 12 + 2 * it + k, upper).wait_send()


def per_device(recording, footprints, pattern, decay, frame_gain, spikes):
    wide = (FR, NCOL * FR)
    vm = pltpu.VMEM
    scratch = [
        vm((PIX, 256), BF16), vm((PIX, FR), BF16), vm((NEU, FR), F32),
        vm((16, FR), F32), vm((1, FR), F32), pltpu.SMEM((K, 32), jnp.int32),
        vm((32, 256, 256), BF16), vm((32, 256, 256), BF16), vm((32, FR, 256), BF16),
        vm(wide, F32), vm(wide, F32), vm(wide, F32), vm(wide, F32), vm(wide, F32),
        vm((2 * FR, NCOL * FR), BF16), vm(wide, F32), vm(wide, F32), vm(wide, F32), vm(wide, F32),
        vm(wide, BF16), vm((FR, (NCOL + 1) * FR), BF16),
        vm((2, FR, FR), F32), vm((FR, FR), F32), vm((FR, 2 * FR), BF16), vm((FR, 2 * FR), BF16),
        vm((ROWS, FR), F32),
        vm((NT, ROWS, FR), F32), vm((NT, ROWS, FR), F32), vm((NT, ROWS, FR), F32),
        vm((NT, ROWS, FR), F32), vm((NT, ROWS, FR), F32),
        vm((ROWS, FR), F32), vm((ROWS, FR), F32),
        vm((2, FR, FR), F32), vm((2, 8, FR), F32),
        vm((2 * ROWS, FR), F32), vm((ROWS, FR), F32), vm((ITERS, 16, FR), F32), vm((ITERS, 32, FR), F32),
        vm((NT, 2 * ROWS, FR), F32), vm((NT, ROWS, FR), F32), vm((ITERS, NT, 16, FR), F32), vm((ITERS, NT, 32, FR), F32),
        vm((2 * ITERS, FR, 2 * FR), F32), vm((2 * ITERS, FR, 2 * FR), F32),
        vm((1 + ITERS, 2, 8, FR), F32), vm((1 + ITERS, 2, NT, 8, FR), F32),
        vm((2 * ITERS, 1, FR), F32),
        vm((ITERS, len(STAGES[0]), 1, FR), F32), vm((ITERS, len(STAGES[1]), 1, FR), F32),
        pltpu.SemaphoreType.DMA((24,)), pltpu.SemaphoreType.DMA((24,)), pltpu.SemaphoreType.DMA((6,)),
    ]
    anywhere = pl.BlockSpec(memory_space=pl.ANY)
    in_vmem = pl.BlockSpec(memory_space=pltpu.VMEM)
    return pl.pallas_call(
        kernel,
        out_shape=(pltpu.VMEM((NEU, FR), F32), pltpu.VMEM((NEU, FR), F32)),
        in_specs=[
            anywhere, anywhere, anywhere, anywhere, anywhere, anywhere,
        ],
        out_specs=(in_vmem, in_vmem),
        scratch_shapes=scratch,
        compiler_params=pltpu.CompilerParams(
            collective_id=0, has_side_effects=True, vmem_limit_bytes=60 * 2**20
        ),
        name="deconvolve",
    )(
        recording, footprints, pattern.T, decay.reshape(16, FR), frame_gain.reshape(1, FR), spikes,
    )


def solution(mesh):
    return jax.shard_map(
        per_device,
        mesh=mesh,
        in_specs=(
            P("tile", "tm"),
            P("tile", None),
            P("tile", None),
            P("tile"),
            P("tm"),
            P("tile", "tm"),
        ),
        out_specs=(P("tile", "tm"), P("tile", "tm")),
        check_vma=False,
    )
```

```python
import functools
import itertools

import jax
import jax.numpy as jnp
from jax import lax
from jax.experimental import pallas as pl
from jax.experimental.pallas import tpu as pltpu
from jax.sharding import PartitionSpec as P

NEU_BLOCK = 64
PIX_BLOCK = 256
K = 4
HB = 2
ITERS = 2

NX, NY, NZ, NC = 4, 4, 8, 2
NT = NX * NC
NTILE = NY * NZ
FR = 128
NCOL = 18
ROWS = 24
NEU = 2048
PIX = 8192
MESH = pl.DeviceIdType.MESH
F32 = jnp.float32
BF16 = jnp.bfloat16


def ring_distance(d, n):
    return min(d, n - d)


def offsets(keep):
    found = []
    for dx, dy, dz, dc in itertools.product(range(NX), range(NY), range(NZ), range(NC)):
        if (dx, dy, dz, dc) != (0, 0, 0, 0) and keep(dx, dy, dz, dc):
            far = ring_distance(dx, NX) + ring_distance(dy, NY) + ring_distance(dz, NZ)
            found.append((-far, dx, dy, dz, dc))
    return [o[1:] for o in sorted(found)]


TM_GROUP = offsets(lambda dx, dy, dz, dc: dy == 0 and dz == 0)
CORE_GROUP = offsets(lambda dx, dy, dz, dc: dx == 0 and dy == 0 and dz == 0)
CHIP_GROUP = offsets(lambda dx, dy, dz, dc: dc == 0)
STAGES = (CORE_GROUP, CHIP_GROUP)


def split_rows(x):
    hi = x.astype(BF16)
    lo = (x - hi.astype(F32)).astype(BF16)
    return hi, lo


def kernel(
    rec_hbm, foot_hbm, pat_hbm, dec_hbm, gain_hbm, spk_hbm,
    out_spk, out_tr,
    foot_raw, rec_raw, spk_raw, decay, fgain, pat, fp, fpt, rec_t,
    cur, grad, fwd, inv, sq, xh, loc, loc2, acc_n, acc_s, val_n, val_s,
    seam, lgb, tri_lo, tri_up, decd, tab_u, tab_e, tab_t, tab_q, tab_c, row_w, row_c,
    halo_spk, halo_dec, msg_a0, msg_a1, msg_cda, msg_cdb, got_a0, got_a1, got_cda, got_cdb,
    msg_b, got_b, msg_h, got_h, msg_e, got_e0, got_e1,
    ss, rs, ls,
):
    tm = lax.axis_index("tm")
    tile = lax.axis_index("tile")
    px, pc = lax.div(tm, NC), lax.rem(tm, NC)
    py, pz = lax.div(tile, NZ), lax.rem(tile, NZ)

    def device_at(o):
        dx, dy, dz, dc = o
        x = lax.rem(px + dx, NX) if dx else px
        c = lax.rem(pc + dc, NC) if dc else pc
        y = lax.rem(py + dy, NY) if dy else py
        z = lax.rem(pz + dz, NZ) if dz else pz
        return (x * NC + c, y * NZ + z)

    upper = (tm, lax.rem(tile + 1, NTILE))
    lower = (tm, lax.rem(tile + NTILE - 1, NTILE))

    group = offsets(lambda *o: o in TM_GROUP or o in CORE_GROUP or o in CHIP_GROUP)
    sides = ((0, 1), (1, NTILE - 1))
    crossed = [(lax.rem(tm + k, NT), lax.rem(tile + by, NTILE)) for _, by in sides for k in range(1, NT, 2)]
    barrier = pltpu.get_barrier_semaphore()
    for o in group:
        pl.semaphore_signal(barrier, inc=1, device_id=device_at(o), device_id_type=MESH)
    for d in crossed:
        pl.semaphore_signal(barrier, inc=1, device_id=d, device_id_type=MESH)

    load_dec = pltpu.make_async_copy(dec_hbm, decay, ls.at[3])
    load_gain = pltpu.make_async_copy(gain_hbm, fgain, ls.at[4])
    load_pat = pltpu.make_async_copy(pat_hbm, pat, ls.at[5])
    load_spk = pltpu.make_async_copy(spk_hbm, spk_raw, ls.at[0])
    load_foot = pltpu.make_async_copy(foot_hbm, foot_raw, ls.at[1])
    load_rec = pltpu.make_async_copy(rec_hbm, rec_raw, ls.at[2])
    for load in (load_dec, load_gain, load_pat, load_spk, load_foot, load_rec):
        load.start()

    def lanes(c, width=128):
        return pl.ds(pl.multiple_of(c * width, width), width)

    row = lax.broadcasted_iota(jnp.int32, (FR, FR), 0)
    col = lax.broadcasted_iota(jnp.int32, (FR, FR), 1)
    low_half = col < NEU_BLOCK
    t_centred = (row - 63).astype(F32)

    lower_tri = (row >= col).astype(BF16)
    upper_tri = (row <= col).astype(BF16)
    tri_lo[:, :FR] = lower_tri
    tri_lo[:, FR:] = lower_tri
    tri_up[:, :FR] = upper_tri
    tri_up[:, FR:] = upper_tri

    load_gain.wait()
    log_fg = jnp.log(fgain[...])
    lg = jnp.sum(jnp.where(row >= col, log_fg, 0.0), axis=1, keepdims=True)
    lg_mid = lg[63:64, :]
    lg_tot = lg[127:128, :]
    lgb[...] = jnp.broadcast_to(lg - lg_mid, (FR, FR))

    msg_a0[...] = jnp.zeros_like(msg_a0)
    msg_a1[...] = jnp.zeros_like(msg_a1)
    msg_cda[...] = jnp.zeros_like(msg_cda)
    msg_cdb[...] = jnp.zeros_like(msg_cdb)
    msg_a0[ROWS + NCOL : ROWS + NCOL + 1, :] = jnp.broadcast_to(lg_tot, (1, FR))
    msg_a0[ROWS + NCOL + 1 : ROWS + NCOL + 2, :] = jnp.broadcast_to(lg_mid, (1, FR))
    decd[...] = jnp.ones_like(decd)
    load_dec.wait()
    decd[1:17, :] = decay[...]

    def prepare(c, d, present, block, own):
        ld = jnp.log1p(d - 1.0)
        gain = jnp.sqrt(1.0 - d * d) * present
        lc = t_centred * ld + lgb[...]
        f = jnp.exp(lc)
        a = gain * jnp.exp(-lc)
        fwd[:, lanes(c)] = f
        inv[:, lanes(c)] = a
        hi, lo = split_rows(a * a)
        s2 = jnp.dot(tri_lo[...], jnp.concatenate([hi, lo], axis=0), preferred_element_type=F32)
        sq[:, lanes(c)] = s2
        if own:
            msg_a0[pl.ds(ROWS + c, 1), :] = s2[FR - 1 : FR, :]
        s = block.T
        cur[:, lanes(c)] = s
        x = a * s
        if own:
            msg_a0[pl.ds(c, 1), :] = jnp.sum(x, axis=0, keepdims=True)
        hi, lo = split_rows(x)
        xh[0:FR, lanes(c)] = hi
        xh[FR : 2 * FR, lanes(c)] = lo

    load_spk.wait()

    def own_column(k, _):
        prepare(k + 1, decd[pl.ds(k + 1, 1), :], 1.0, spk_raw[pl.ds(pl.multiple_of(k * FR, FR), FR), :], True)
        return 0

    lax.fori_loop(0, 16, own_column, 0, unroll=4)

    def names(q, k, v):
        return jnp.where(pat[k, q] - q == v, 1.0, 0.0)

    def sources(q):
        own = [[names(q, k, v) for k in range(K)] for v in (0, 2, 4)]
        return own + [[1.0 - own[0][k] - own[1][k] - own[2][k] for k in range(K)]]

    def is_one(q):
        return sum(names(q, k, 1) for k in range(K))

    load_pat.wait()
    load_foot.wait()

    def arrange(q, _):
        at = pl.ds(pl.multiple_of(q * PIX_BLOCK, PIX_BLOCK), PIX_BLOCK)
        turned = foot_raw[at, :].T
        chunks = [turned[k * NEU_BLOCK : (k + 1) * NEU_BLOCK, :] for k in range(K)]
        for s, weights in enumerate(sources(q)):
            mixed = sum(chunks[k] * jnp.full((1, PIX_BLOCK), weights[k], F32).astype(BF16) for k in range(K))
            fpt[q, s * NEU_BLOCK : (s + 1) * NEU_BLOCK, :] = mixed
        fp[q] = fpt[q].T
        return 0


    lax.fori_loop(0, 4, arrange, 0, unroll=4)

    pl.semaphore_wait(barrier, len(group) + len(crossed))

    def remote(src, dst, k, device):
        return pltpu.make_async_remote_copy(
            src_ref=src, dst_ref=dst, send_sem=ss.at[k], recv_sem=rs.at[k],
            device_id=device, device_id_type=MESH,
        )

    def group_send(src, got, k):
        for r in range(1, NT):
            remote(src, got.at[r - 1], k, (lax.rem(tm + r, NT), tile)).start()
        got[NT - 1] = src[...]

    def group_wait(got, k):
        part = got.at[pl.ds(0, NT - 1)]
        remote(part, part, k, upper).wait_recv()

    def group_sent(got, k):
        part = got.at[pl.ds(0, NT - 1)]
        remote(part, part, k, upper).wait_send()

    def slot_of(j):
        return lax.rem(tm - j + NT - 1, NT)

    def wide_send(src, got, k):
        for side, by in sides:
            for r in range(NT):
                to = (lax.rem(tm + r, NT), lax.rem(tile + by, NTILE))
                remote(src.at[side], got.at[side, (r + NT - 1) % NT], k + side, to).start()

    def wide_wait(got, k):
        for side, _ in sides:
            remote(got.at[side], got.at[side], k + side, upper).wait_recv()

    def wide_sent(got, k):
        for side, _ in sides:
            remote(got.at[side], got.at[side], k + side, upper).wait_send()

    msg_h[0] = jnp.zeros_like(msg_h[0])
    msg_h[0, 0, 0:1, :] = msg_a0[16:17, :]
    msg_h[0, 0, 1:2, :] = msg_a0[ROWS + 16 : ROWS + 17, :]
    msg_h[0, 1, 0:1, :] = msg_a0[1:2, :]
    msg_h[0, 1, 1:2, :] = msg_a0[ROWS + 1 : ROWS + 2, :]
    wide_send(msg_h.at[0], got_h.at[0], 16)
    group_send(msg_a0, got_a0, 4)
    halo = [
        remote(spk_hbm.at[pl.ds(NEU - FR, FR), :], halo_spk.at[0], 0, upper),
        remote(spk_hbm.at[pl.ds(0, FR), :], halo_spk.at[1], 1, lower),
        remote(decay.at[pl.ds(8, 8), :], halo_dec.at[0], 2, upper),
        remote(decay.at[pl.ds(0, 8), :], halo_dec.at[1], 3, lower),
    ]
    for copy in halo:
        copy.start()

    lax.fori_loop(4, 32, arrange, 0, unroll=4)

    load_rec.wait()

    def turn(q, _):
        rec_t[q] = rec_raw[pl.ds(pl.multiple_of(q * PIX_BLOCK, PIX_BLOCK), PIX_BLOCK), :].T
        return 0

    lax.fori_loop(0, 32, turn, 0, unroll=8)

    for copy in halo:
        copy.wait_recv()
    decd[0:1, :] = halo_dec[0, 7:8, :]
    decd[17:18, :] = halo_dec[1, 0:1, :]
    has_lower = jnp.where(tile > 0, 1.0, 0.0)
    has_upper = jnp.where(tile < NTILE - 1, 1.0, 0.0)
    prepare(0, decd[0:1, :], has_lower, halo_spk[0], False)
    prepare(17, decd[17:18, :], has_upper, halo_spk[1], False)

    def cumulate(tri, out, first=0, last=NCOL // 2):
        def body(c, _):
            at = lanes(c, 256)
            out[:, at] = jnp.dot(tri[...], xh[:, at], preferred_element_type=F32)
            return 0

        lax.fori_loop(first, last, body, 0, unroll=last - first)

    def put_column(c, y, before):
        val_n[:, lanes(c)] = y.astype(BF16)
        turned = pltpu.roll(y, NEU_BLOCK, 1)
        val_s[:, lanes(c)] = jnp.where(low_half, before, turned).astype(BF16)
        return turned

    def put_moved(c, turned, after):
        val_s[:, lanes(c + 1)] = jnp.where(low_half, turned, after).astype(BF16)

    nothing = jnp.zeros((FR, FR), F32)

    low_row = lax.broadcasted_iota(jnp.int32, (1, FR), 1) < NEU_BLOCK
    m_lo = jnp.where(low_row, 1.0, 0.0).astype(BF16)
    m_hi = jnp.where(low_row, 0.0, 1.0).astype(BF16)

    def pick(i):
        n0, n1, n2 = (val_n[:, lanes(i + k)] for k in range(3))
        s0, s1, s2 = (val_s[:, lanes(i + 1 + k)] for k in range(3))
        one_e, one_o = is_one(2 * i), is_one(2 * i + 1)

        def pair(x0, x1, x2, y, one):
            a = x0 * m_lo + y * m_hi
            first = jnp.where(low_row, 0.0, one).astype(BF16)
            second = jnp.where(low_row, 0.0, 1.0 - one).astype(BF16)
            b = x2 * m_lo + x0 * first + x1 * second
            return jnp.concatenate([a, b], axis=1)

        return pair(n0, n1, n2, s0, one_e), pair(s0, s1, s2, n1, one_o), one_e, one_o

    def model(i):
        even, odd, one_e, one_o = pick(i)
        y_e = jnp.dot(even, fpt[2 * i], preferred_element_type=F32)
        y_o = jnp.dot(odd, fpt[2 * i + 1], preferred_element_type=F32)
        return y_e, y_o, one_e, one_o

    def residual_step(i):
        y_e, y_o, one_e, one_o = model(i)
        r_e = (y_e - rec_t[2 * i].astype(F32)).astype(BF16)
        r_o = (y_o - rec_t[2 * i + 1].astype(F32)).astype(BF16)
        c = jnp.dot(r_e, fp[2 * i], preferred_element_type=F32)
        d = jnp.dot(r_o, fp[2 * i + 1], preferred_element_type=F32)
        ca, cb, da, db = c[:, :FR], c[:, FR:], d[:, :FR], d[:, FR:]
        acc_n[:, lanes(i)] += jnp.where(low_half, ca, cb * one_e)
        acc_s[:, lanes(i)] += jnp.where(low_half, da, ca + db * one_o)
        acc_n[:, lanes(i + 1)] += jnp.where(low_half, 0.0, cb * (1.0 - one_e) + da)
        acc_s[:, lanes(i + 1)] += jnp.where(low_half, 0.0, db * (1.0 - one_o))
        acc_n[:, lanes(i + 2)] += jnp.where(low_half, cb, 0.0)
        acc_s[:, lanes(i + 2)] += jnp.where(low_half, db, 0.0)

    def total_column(c, first=False):
        before = 0.0 if first else acc_s[:, lanes(c - 1)]
        return acc_n[:, lanes(c)] + pltpu.roll(jnp.where(low_half, acc_s[:, lanes(c)], before), NEU_BLOCK, 1)

    step = None
    for it in range(ITERS):
        msg_a, got_a, sem_a = (msg_a0, got_a0, 4) if it == 0 else (msg_a1, got_a1, 5)
        if it > 0:

            def update(c, _):
                at = lanes(c, 256)
                new = jnp.maximum(cur[:, at] - step * grad[:, at], 0.0)
                cur[:, at] = new
                x = inv[:, at] * new
                sums = jnp.sum(x, axis=0, keepdims=True)
                msg_a1[pl.ds(2 * c, 1), :] = sums[:, :FR]
                msg_a1[pl.ds(2 * c + 1, 1), :] = sums[:, FR:]
                hi, lo = split_rows(x)
                xh[0:FR, at] = hi
                xh[FR : 2 * FR, at] = lo
                return 0

            lax.fori_loop(0, NCOL // 2, update, 0, unroll=3)
            group_send(msg_a, got_a, sem_a)
        cumulate(tri_lo, loc)
        acc_n[...] = jnp.zeros_like(acc_n)
        acc_s[...] = jnp.zeros_like(acc_s)
        group_wait(got_a, sem_a)
        if it == 0:
            wide_wait(got_h.at[0], 16)
            for k in range(NT):
                for part, at in ((0, 0), (1, ROWS)):
                    got_a0[k, at : at + 1, :] = has_lower * got_h[0, 0, k, part : part + 1, :]
                    got_a0[k, at + 17 : at + 18, :] = has_upper * got_h[0, 1, k, part : part + 1, :]
            ld = jnp.log1p(decd[...] - 1.0)
            run = None
            for j in range(NT):
                tab = got_a0.at[slot_of(j)]
                tot = tab[ROWS + NCOL : ROWS + NCOL + 1, :]
                mid = tab[ROWS + NCOL + 1 : ROWS + NCOL + 2, :]
                tab_u[j] = jnp.exp(64.0 * ld + (tot - mid))
                tab_e[j] = jnp.exp(64.0 * ld + mid)
                tab_t[j] = jnp.exp(128.0 * ld + tot)
                tab_q[j] = tab_u[j] * tab[ROWS : 2 * ROWS, :]
            run = tab_e[tm]
            for j in range(NT - 1, -1, -1):
                active = j < tm
                tab_c[j] = jnp.where(active, run * tab_u[j], 0.0)
                run = jnp.where(active, run * tab_t[j], run)
        carry = jnp.zeros((ROWS, FR), F32)
        for j in range(NT):
            carry = carry + tab_c[j] * got_a[slot_of(j), 0:ROWS, :]
        row_c[...] = carry

        def traces_of(c):
            y = fwd[:, lanes(c)] * (loc[:, lanes(c)] + row_c[pl.ds(c, 1), :])
            if it == ITERS - 1:
                loc[:, lanes(c)] = y
            return y

        def put_trace(c, before):
            return put_column(c, traces_of(c), before)

        def put_and_step(c, before):
            turned = put_trace(c, before)
            residual_step(c - 3)
            return turned

        def step_only(i, _):
            residual_step(i)
            return 0

        seam[0] = lax.fori_loop(0, 5, put_trace, nothing, unroll=5)
        lax.fori_loop(0, 2, step_only, 0, unroll=2)
        seam[1] = put_trace(14, nothing)
        put_moved(17, lax.fori_loop(15, NCOL, put_trace, seam[1], unroll=3), nothing)
        lax.fori_loop(14, 16, step_only, 0, unroll=2)
        msg_b[2 * it, :, :FR] = total_column(0, first=True)
        msg_b[2 * it, :, FR:] = total_column(1)
        msg_b[2 * it + 1, :, :FR] = total_column(16)
        msg_b[2 * it + 1, :, FR:] = total_column(17)
        to_low = remote(msg_b.at[2 * it], got_b.at[2 * it], 6 + 2 * it, lower)
        to_up = remote(msg_b.at[2 * it + 1], got_b.at[2 * it + 1], 7 + 2 * it, upper)
        to_low.start()
        to_up.start()

        parts_cd = ((msg_cda, got_cda, 0, 8, 10 + it), (msg_cdb, got_cdb, 8, 16, 22 + it))

        def sum_column(c, x, part):
            msg, _, base, n, _ = parts_cd[part]
            msg[it, pl.ds(c - base, 1), :] = jnp.sum(x, axis=0, keepdims=True)
            msg[it, pl.ds(n + c - base, 1), :] = jnp.sum(x * sq[:, lanes(c)], axis=0, keepdims=True)

        def split_column(c, x):
            hi, lo = split_rows(x)
            xh[0:FR, lanes(c)] = hi
            xh[FR : 2 * FR, lanes(c)] = lo

        for c, part, half in ((0, 2 * it, 0), (1, 2 * it, 1), (16, 2 * it + 1, 0), (17, 2 * it + 1, 1)):
            sum_column(c, fwd[:, lanes(c)] * msg_b[part, :, half * FR : (half + 1) * FR], part - 2 * it)
        msg_h[1 + it] = jnp.zeros_like(msg_h[1 + it])
        msg_h[1 + it, 0, 0:2, :] = msg_cdb[it, 8:10, :]
        msg_h[1 + it, 0, 2:4, :] = msg_cdb[it, 24:26, :]
        msg_h[1 + it, 1, 0:2, :] = msg_cda[it, 0:2, :]
        msg_h[1 + it, 1, 2:4, :] = msg_cda[it, 8:10, :]
        wide_send(msg_h.at[1 + it], got_h.at[1 + it], 18 + 2 * it)

        def inner_columns(first, last, part):
            def inner_column(c, _):
                x = fwd[:, lanes(c)] * total_column(c)
                sum_column(c, x, part)
                split_column(c, x)
                return 0

            lax.fori_loop(first, last, inner_column, 0, unroll=last - first)
            msg, got, _, _, k = parts_cd[part]
            group_send(msg.at[it], got.at[it], k)

        before = lax.fori_loop(5, 11, put_and_step, seam[0], unroll=6)
        inner_columns(2, 8, 0)
        put_moved(13, lax.fori_loop(11, 14, put_and_step, before, unroll=3), seam[1])
        lax.fori_loop(11, 14, step_only, 0, unroll=3)
        inner_columns(8, 16, 1)
        cumulate(tri_up, loc2, 1, 8)
        to_low.wait_recv()
        to_up.wait_recv()
        for c, part, present in ((0, 2 * it + 1, has_lower), (16, 2 * it, has_upper)):
            for half in range(2):
                at = slice(half * FR, (half + 1) * FR)
                mine = msg_b[2 * it if c == 0 else 2 * it + 1, :, at]
                split_column(c + half, fwd[:, lanes(c + half)] * (mine + present * got_b[part, :, at]))
        cumulate(tri_up, loc2, 0, 1)
        cumulate(tri_up, loc2, 8, 9)

        def square_part(c, _):
            at = lanes(c, 256)
            a = inv[:, at]
            hi, lo = split_rows(a * a * loc2[:, at])
            both = jnp.concatenate([hi, lo], axis=0)
            grad[:, at] = jnp.dot(tri_lo[...], both, preferred_element_type=F32)
            return 0

        lax.fori_loop(0, NCOL // 2, square_part, 0, unroll=9)
        def carries(part):
            _, got, base, n, k = parts_cd[part]
            group_wait(got.at[it], k)
            at = part * 8
            present = (has_lower, has_upper)[part]
            for k in range(NT):
                got[it, k, at : at + 2, :] += present * got_h[1 + it, part, k, 0:2, :]
                got[it, k, n + at : n + at + 2, :] += present * got_h[1 + it, part, k, 2:4, :]
            rows = slice(base, base + n)
            w = jnp.zeros((n, FR), F32)
            mine = w
            carry = w
            for j in range(NT - 1, -1, -1):
                at = slot_of(j)
                mine = jnp.where(tm == j, w, mine)
                carry = carry + tab_c[j, rows, :] * (got[it, at, n : 2 * n, :] + tab_q[j, rows, :] * w)
                w = tab_e[j, rows, :] * got[it, at, 0:n, :] + tab_t[j, rows, :] * w
            row_w[rows, :] = tab_u[tm, rows, :] * mine
            row_c[rows, :] = carry

        wide_wait(got_h.at[1 + it], 18 + 2 * it)
        carries(0)

        def direction_of(c):
            at = lanes(c)
            return fwd[:, at] * (grad[:, at] + sq[:, at] * row_w[pl.ds(c, 1), :] + row_c[pl.ds(c, 1), :])

        def gradient_column(c):
            at = lanes(c)
            g = inv[:, at] * (loc2[:, at] + row_w[pl.ds(c, 1), :])
            grad[:, at] = g
            return g

        def image_step(i, sums):
            g_sum, p_sum = sums
            y_e, y_o, _, _ = model(i)
            p = y_e * y_e + y_o * y_o
            p_sum = p_sum + jnp.sum(p.reshape(16, 8, 256), axis=0)
            g = gradient_column(i + 1)
            g_sum = g_sum + jnp.sum((g * g).reshape(16, 8, FR), axis=0)
            return g_sum, p_sum

        def put_direction(c, before):
            return put_column(c, direction_of(c), before)

        def put_and_image(c, carried):
            before, g_sum, p_sum = carried
            turned = put_direction(c, before)
            return (turned,) + image_step(c - 3, (g_sum, p_sum))

        before = lax.fori_loop(0, 3, put_direction, nothing, unroll=3)
        carried = (before, jnp.zeros((8, FR), F32), jnp.zeros((8, 2 * FR), F32))
        carried = lax.fori_loop(3, 8, put_and_image, carried, unroll=5)
        carries(1)
        before, g_sum, p_sum = lax.fori_loop(8, NCOL, put_and_image, carried, unroll=10)
        put_moved(17, before, nothing)
        g_sum, p_sum = image_step(15, (g_sum, p_sum))
        g_row = jnp.sum(g_sum, axis=0, keepdims=True)
        p_row = jnp.sum(p_sum[:, :FR] + p_sum[:, FR:], axis=0, keepdims=True)
        total = jnp.where(
            low_row, g_row + pltpu.roll(g_row, NEU_BLOCK, 1), p_row + pltpu.roll(p_row, NEU_BLOCK, 1)
        )
        for k, (stage, got_e) in enumerate(zip(STAGES, (got_e0, got_e1))):
            msg_e[2 * it + k] = total
            n = len(stage)
            for i, o in enumerate(stage):
                remote(msg_e.at[2 * it + k], got_e.at[it, i], 12 + 2 * it + k, device_at(o)).start()
            if k == 0:
                if it < ITERS - 1:
                    gradient_column(0)
                    gradient_column(17)
            elif it == ITERS - 1:

                def turn_out(c, _):
                    at = lanes(c + 1)
                    to = pl.ds(pl.multiple_of(c * FR, FR), FR)
                    out_tr[to, :] = loc[:, at].T
                    spk_raw[to, :] = cur[:, at].T
                    rec32 = grad[:, at].T
                    out_spk[to, :] = rec32
                    return 0

                lax.fori_loop(0, 16, turn_out, 0, unroll=4)
            everything = got_e.at[it]
            remote(everything, everything, 12 + 2 * it + k, upper).wait_recv()
            parts = [total] + [got_e[it, i] for i in range(n)]
            while len(parts) > 1:
                parts = [a + b for a, b in zip(parts[::2], parts[1::2])] + parts[len(parts) // 2 * 2 :]
            total = parts[0]
        grad_sq = jnp.sum(jnp.where(low_row, total, 0.0), axis=1, keepdims=True)
        image_sq = jnp.sum(jnp.where(low_row, 0.0, total), axis=1, keepdims=True)
        step = grad_sq / (image_sq + 1e-06)

    def finish(c, _):
        to = pl.ds(pl.multiple_of(c * 256, 256), 256)
        out_spk[to, :] = jnp.maximum(spk_raw[to, :] - step * out_spk[to, :], 0.0)
        return 0

    lax.fori_loop(0, 8, finish, 0, unroll=4)

    for copy in halo:
        copy.wait_send()
    group_sent(got_a0, 4)
    group_sent(got_a1, 5)
    for k in range(1 + ITERS):
        wide_sent(got_h.at[k], 16 + 2 * k)
    for it in range(ITERS):
        remote(msg_b.at[2 * it], got_b.at[2 * it], 6 + 2 * it, lower).wait_send()
        remote(msg_b.at[2 * it + 1], got_b.at[2 * it + 1], 7 + 2 * it, upper).wait_send()
        group_sent(got_cda.at[it], 10 + it)
        group_sent(got_cdb.at[it], 22 + it)
        for k, got_e in enumerate((got_e0, got_e1)):
            everything = got_e.at[it]
            remote(everything, everything, 12 + 2 * it + k, upper).wait_send()


def per_device(recording, footprints, pattern, decay, frame_gain, spikes):
    wide = (FR, NCOL * FR)
    vm = pltpu.VMEM
    scratch = [
        vm((PIX, 256), BF16), vm((PIX, FR), BF16), vm((NEU, FR), F32),
        vm((16, FR), F32), vm((1, FR), F32), pltpu.SMEM((K, 32), jnp.int32),
        vm((32, 256, 256), BF16), vm((32, 256, 256), BF16), vm((32, FR, 256), BF16),
        vm(wide, F32), vm(wide, F32), vm(wide, F32), vm(wide, F32), vm(wide, F32),
        vm((2 * FR, NCOL * FR), BF16), vm(wide, F32), vm(wide, F32), vm(wide, F32), vm(wide, F32),
        vm(wide, BF16), vm((FR, (NCOL + 1) * FR), BF16),
        vm((2, FR, FR), F32), vm((FR, FR), F32), vm((FR, 2 * FR), BF16), vm((FR, 2 * FR), BF16),
        vm((ROWS, FR), F32),
        vm((NT, ROWS, FR), F32), vm((NT, ROWS, FR), F32), vm((NT, ROWS, FR), F32),
        vm((NT, ROWS, FR), F32), vm((NT, ROWS, FR), F32),
        vm((ROWS, FR), F32), vm((ROWS, FR), F32),
        vm((2, FR, FR), F32), vm((2, 8, FR), F32),
        vm((2 * ROWS, FR), F32), vm((ROWS, FR), F32), vm((ITERS, 16, FR), F32), vm((ITERS, 32, FR), F32),
        vm((NT, 2 * ROWS, FR), F32), vm((NT, ROWS, FR), F32), vm((ITERS, NT, 16, FR), F32), vm((ITERS, NT, 32, FR), F32),
        vm((2 * ITERS, FR, 2 * FR), F32), vm((2 * ITERS, FR, 2 * FR), F32),
        vm((1 + ITERS, 2, 8, FR), F32), vm((1 + ITERS, 2, NT, 8, FR), F32),
        vm((2 * ITERS, 1, FR), F32),
        vm((ITERS, len(STAGES[0]), 1, FR), F32), vm((ITERS, len(STAGES[1]), 1, FR), F32),
        pltpu.SemaphoreType.DMA((24,)), pltpu.SemaphoreType.DMA((24,)), pltpu.SemaphoreType.DMA((6,)),
    ]
    anywhere = pl.BlockSpec(memory_space=pl.ANY)
    in_vmem = pl.BlockSpec(memory_space=pltpu.VMEM)
    return pl.pallas_call(
        kernel,
        out_shape=(pltpu.VMEM((NEU, FR), F32), pltpu.VMEM((NEU, FR), F32)),
        in_specs=[
            anywhere, anywhere, anywhere, anywhere, anywhere, anywhere,
        ],
        out_specs=(in_vmem, in_vmem),
        scratch_shapes=scratch,
        compiler_params=pltpu.CompilerParams(
            collective_id=0, has_side_effects=True, vmem_limit_bytes=60 * 2**20
        ),
        name="deconvolve",
    )(
        recording, footprints, pattern.T, decay.reshape(16, FR), frame_gain.reshape(1, FR), spikes,
    )


def solution(mesh):
    return jax.shard_map(
        per_device,
        mesh=mesh,
        in_specs=(
            P("tile", "tm"),
            P("tile", None),
            P("tile", None),
            P("tile"),
            P("tm"),
            P("tile", "tm"),
        ),
        out_specs=(P("tile", "tm"), P("tile", "tm")),
        check_vma=False,
    )
```
